256 devices in a mesh: rep: 32 (over z_hi, y, core), shard: 8 (over x, z_lo).
Axes of the slice: x: 4, y: 4, z: 8 (z_hi: 4, z_lo: 2; z = z_hi * 2 + z_lo), core: 2. Of those that a mesh axis runs over, the one named last changes fastest.
Arguments:
- tokens: bfloat16 [32768, 2048], P(('rep', 'shard')), may hold values from -6 to 6
- routes: int32 [32768, 2], P(('rep', 'shard')), may hold values from 0 to 7, all different within a row; in each aligned block of 128 rows (0 to 127, 128 to 255, ...) at most 48 rows name the same one
- route_weight: float32 [32768, 2], P(('rep', 'shard')), may hold values from 0.2 to 1
- w_gate: bfloat16 [8, 2048, 768], P('shard'), may hold values from -0.125 to 0.125
- w_up: bfloat16 [8, 2048, 768], P('shard'), may hold values from -0.125 to 0.125
- w_down: bfloat16 [8, 768, 2048], P('shard'), may hold values from -0.21875 to 0.21875
- pseudo_grad: float32 [32, 768, 2048], P('rep', 'shard'), may hold values from -5400 to 5400
- global_params: float32 [768, 2048], P('shard'), may hold values from -6 to 6
- momentum: float32 [768, 2048], P('shard', 'rep'), may hold values from -3 to 3
- local_params: bfloat16 [32, 768, 2048], P('rep', 'shard'), may hold values from -6 to 6
Outputs:
- moe_out: bfloat16 [32768, 2048], P(('rep', 'shard'))
- momentum_next: float32 [768, 2048], P('shard', 'rep')
- local_next: bfloat16 [32, 768, 2048], P('rep', 'shard')
The draws below stay inside these ranges and needn't reach their ends.
Inputs may be any that keep to these rules, and one draw needn't show every extreme that they name: `routes`: each token names 2 different experts. Within the rows of one device no expert is named by more than 48 rows, and on some device one is named by exactly 48.
All inputs are finite; a program needn't handle non-finite values.
Results may differ from the reference program's by a relative error of at most 0.0057.
Values may be sent and summed in bfloat16 or wider, within the bound.
No kernel may reach another device: no remote copies, remote signals or barrier semaphores. Data moves between devices by JAX's collectives and lax.ppermute only.
A program may use at most 64 MiB of HBM per device.

```python
import math
import jax
import jax.numpy as jnp
import numpy as np
from jax import lax

D = 2048
FF_WIN = 768
EXPERTS = 8
TOPK = 2
TOK_DEV = 128
CAP = 48
REPLICAS = 32
TOKENS = 32768
FRAG_ROWS = 768


def draw_pseudo_grad(key, part):
    key = jax.random.fold_in(key, 11)
    key_rows, key_cols, key_own = jax.random.split(key, 3)
    rising = 1.0 + 2.0 * jnp.arange(FRAG_ROWS, dtype=jnp.float32) / max(FRAG_ROWS - 1, 1)
    row_scale = jnp.exp(jax.random.uniform(key_rows, (FRAG_ROWS,), jnp.float32, 0.0, math.log(10.0))) * rising
    col_scale = jnp.exp(jax.random.uniform(key_cols, (D,), jnp.float32, 0.0, math.log(10.0)))
    own_part = jax.random.normal(key_own, (REPLICAS, FRAG_ROWS, D), jnp.float32)
    base = jnp.clip(own_part, -6.0, 6.0)
    return (base * row_scale[None, :, None] * col_scale[None, None, :]).astype(jnp.float32)


def block_scale(own_key, dims, pieces, least, largest):
    def one(dim, parts):
        draws = jax.random.uniform(jax.random.fold_in(jax.random.fold_in(own_key, 6), dim), (parts,), jnp.float32, least / len(pieces), largest / len(pieces))
        return jnp.repeat(jnp.exp(draws), dims[dim] // parts).reshape((-1,) + (1,) * (len(dims) - dim - 1))

    loudness = one(*pieces[0])
    for cut in pieces[1:]:
        loudness = loudness * one(*cut)
    return loudness


def shared_out(key, own, number, rows, amount, top, limit, lean):
    order = jax.random.permutation(key, amount)
    heavy_load, ordinary = shares(amount, rows * top, limit, lean, True), shares(amount, rows * top, limit, lean, False)
    places = jnp.arange(amount)

    def named(tallies, rotation):
        used = int((tallies > 0).sum())
        fixed = max(1, used // 4)
        passed = fixed + (places - fixed + rotation * (used - fixed)) % max(1, amount - fixed)
        return jnp.zeros((amount,), jnp.int32).at[order[jnp.where(places < fixed, places, passed)]].set(jnp.asarray(tallies, jnp.int32))

    tallies = jnp.where(number % 4 == 0, named(heavy_load, number // 4), named(ordinary, number - number // 4 - 1))
    mixed = jax.random.permutation(jax.random.fold_in(own, 3), amount)
    giver, receiver = mixed[0:amount // 2 * 2:2], mixed[1:amount // 2 * 2:2]
    room = jnp.minimum(tallies[giver] - 1, limit - tallies[receiver]) // 2
    room = jnp.where((giver == order[0]) | (receiver == order[0]) | (tallies[receiver] == 0), 0, jnp.maximum(room, 0))
    passed = jax.random.randint(jax.random.fold_in(own, 4), (amount // 2,), 0, 1 << 20) % (room + 1)
    tallies = tallies.at[giver].add(-passed).at[receiver].add(passed)
    labels = jnp.searchsorted(jnp.cumsum(tallies), jnp.arange(rows * top), side="right").astype(jnp.int32)
    table = labels.reshape(top, rows).T
    table = table[jax.random.permutation(jax.random.fold_in(own, 1), rows)]
    rotation = jax.random.randint(jax.random.fold_in(own, 2), (rows, 1), 0, top)
    return jnp.take_along_axis(table, (jnp.arange(top)[None, :] + rotation) % top, axis=1)


def shares(amount, total, limit, skew, full):
    portions = [(1 << 20) // math.isqrt(rank ** skew) + 1 for rank in range(1, amount + 1)]
    largest = limit if full else min(limit, max(-(-total // amount), total * portions[0] // sum(portions)))
    least = 1 if total - largest >= amount - 1 else 0
    given, rest = [largest] + [least] * (amount - 1), total - largest - least * (amount - 1)
    while rest > 0:
        candidates = [i for i in range(1, amount) if given[i] < largest] or [i for i in range(1, amount) if given[i] < limit]
        mass, budget = sum([portions[i] for i in candidates]), rest
        for i in candidates:
            extra = min(limit - given[i], max(1, budget * portions[i] // mass), rest)
            given[i] = given[i] + extra
            rest = rest - extra
    return np.array(given)


def centred(rng, dims, spread, limit, shards=(), held_as=jnp.bfloat16):
    loudness = block_scale(rng, dims, shards, -0.22, 0.18) if shards else 1.0
    values = jax.random.normal(rng, dims, jnp.float32) * spread * loudness
    return jnp.minimum(jnp.maximum(values, -limit), limit).astype(held_as)


def setup_inputs(seed: int = 0) -> dict:
    seeds = jax.random.split(jax.random.key(seed), 11)
    tokens = centred(seeds[0], (TOKENS, D), 1.0, 6.0, ((0, 256),))
    routes_keys = jax.random.split(jax.random.fold_in(seeds[1], 1), TOKENS // TOK_DEV)
    routes_turns = jax.random.permutation(jax.random.fold_in(seeds[1], 3), TOKENS // TOK_DEV)
    routes = jax.vmap(lambda own, number: shared_out(jax.random.fold_in(seeds[1], 2), own, number, TOK_DEV, EXPERTS, TOPK, CAP, 1))(routes_keys, routes_turns).reshape((TOKENS, TOPK))
    route_weight = jnp.clip(0.2 + 0.8 * jax.random.uniform(seeds[2], (TOKENS, TOPK), jnp.float32) ** block_scale(seeds[2], (TOKENS, TOPK), ((0, 256),), -0.2, 0.2), 0.2, 1.0)
    w_gate = centred(seeds[3], (EXPERTS, D, FF_WIN), D ** -0.5, 0.125, ((0, 8),))
    w_up = centred(seeds[4], (EXPERTS, D, FF_WIN), D ** -0.5, 0.125, ((0, 8),))
    w_down = centred(seeds[5], (EXPERTS, FF_WIN, D), FF_WIN ** -0.5, 0.21875, ((0, 8),))
    pseudo_grad = draw_pseudo_grad(jax.random.fold_in(seeds[10], 71), 0)
    global_params = centred(seeds[7], (FRAG_ROWS, D), 1.0, 6.0, ((0, 8),), jnp.float32)
    momentum = centred(seeds[8], (FRAG_ROWS, D), 0.5, 3.0, ((0, 8), (1, 32)), jnp.float32)
    local_params = centred(seeds[9], (REPLICAS, FRAG_ROWS, D), 1.0, 6.0, ((0, 32), (1, 8)))
    return {"tokens": tokens, "routes": routes, "route_weight": route_weight, "w_gate": w_gate, "w_up": w_up, "w_down": w_down, "pseudo_grad": pseudo_grad, "global_params": global_params, "momentum": momentum, "local_params": local_params}


outer_momentum = 0.9
outer_rate = 0.7
merge_weight = 0.5
clip_epsilon = 1e-06

def slot_table(flat_routes):
    one_hot = (flat_routes[:, None] == jnp.arange(EXPERTS, dtype=jnp.int32)[None, :]).astype(jnp.int32)
    earlier = jnp.cumsum(one_hot, axis=0) - one_hot
    position = lax.optimization_barrier(jnp.sum(earlier * one_hot, axis=1))
    return (flat_routes * CAP + position).astype(jnp.int32)

def expert_apply(operands):
    expert_rows, gate_mat, up_mat, down_mat = operands
    gate = jnp.dot(expert_rows, gate_mat, preferred_element_type=jnp.float32)
    upward = jnp.dot(expert_rows, up_mat, preferred_element_type=jnp.float32)
    hidden = (jax.nn.silu(gate) * upward).astype(jnp.bfloat16)
    return jnp.dot(hidden, down_mat, preferred_element_type=jnp.float32).astype(jnp.bfloat16)

def reference(tokens, routes, route_weight, w_gate, w_up, w_down, pseudo_grad, global_params, momentum, local_params):
    blocks = TOKENS // TOK_DEV
    feat_width = tokens.shape[1]
    block_tokens = tokens.reshape(blocks, TOK_DEV, feat_width)
    block_routes = routes.reshape(blocks, TOK_DEV * TOPK)
    slot_index = jax.vmap(slot_table)(block_routes)
    sources = jnp.repeat(block_tokens, TOPK, axis=1)
    empty = jnp.zeros((blocks, EXPERTS * CAP, feat_width), tokens.dtype)
    buffer = jax.vmap(lambda base, where, values: base.at[where].set(values))(empty, slot_index, sources)
    per_expert = buffer.reshape(blocks, EXPERTS, CAP, feat_width).transpose(1, 0, 2, 3).reshape(EXPERTS, blocks * CAP, feat_width)
    expert_out = lax.map(expert_apply, (per_expert, w_gate, w_up, w_down))
    returned = expert_out.reshape(EXPERTS, blocks, CAP, feat_width).transpose(1, 0, 2, 3).reshape(blocks, EXPERTS * CAP, feat_width)
    picked = jax.vmap(lambda table, where: table[where])(returned, slot_index)
    picked = picked.reshape(blocks, TOK_DEV, TOPK, feat_width).astype(jnp.float32)
    weights = route_weight.reshape(blocks, TOK_DEV, TOPK, 1)
    moe_out = lax.optimization_barrier(jnp.sum(weights * picked, axis=2)).reshape(TOKENS, feat_width).astype(jnp.bfloat16)
    mean_delta = lax.optimization_barrier(jnp.sum(pseudo_grad, axis=0)) / REPLICAS
    mean_square = jnp.mean(mean_delta * mean_delta)
    clip_factor = jnp.minimum(1.0, lax.rsqrt(mean_square + clip_epsilon))
    clipped = clip_factor * mean_delta
    momentum_next = outer_momentum * momentum + clipped
    global_next = global_params - outer_rate * (outer_momentum * momentum_next + clipped)
    local_next = (merge_weight * local_params.astype(jnp.float32) + (1.0 - merge_weight) * global_next[None]).astype(jnp.bfloat16)
    return (moe_out, momentum_next, local_next)
```

```python
import jax
import jax.numpy as jnp
from jax import lax
from jax.experimental import pallas as pl
from jax.experimental.pallas import tpu as pltpu
from jax.sharding import Mesh
from jax.sharding import PartitionSpec as P

f32 = jnp.float32
bf16 = jnp.bfloat16

outer_momentum = 0.9
outer_rate = 0.7
merge_weight = 0.5
clip_epsilon = 1e-06

EXPERTS = 8
REP = ("zh", "y", "c")
SHARD = ("x", "zl")
VMEM_LIMIT = 48 * 1024 * 1024


def params(**more):
    return pltpu.CompilerParams(vmem_limit_bytes=VMEM_LIMIT, **more)


def whole(count):
    return [pl.BlockSpec(memory_space=pltpu.VMEM)] * count


def slots(routes, tokens, capacity):
    ids = lax.broadcasted_iota(jnp.int32, (EXPERTS, tokens), 0)
    named = jnp.logical_or(routes[0:1, :] == ids, routes[1:2, :] == ids)
    before = lax.broadcasted_iota(jnp.int32, (tokens, tokens), 0) < lax.broadcasted_iota(
        jnp.int32, (tokens, tokens), 1
    )
    place = jnp.dot(
        named.astype(f32).astype(bf16), before.astype(f32).astype(bf16), preferred_element_type=f32
    )
    return jnp.where(named, place.astype(jnp.int32), capacity)


def dispatch_kernel(routes_ref, tokens_ref, out_ref):
    tokens = tokens_ref.shape[0]
    capacity = out_ref.shape[1]
    place = slots(routes_ref[...], tokens, capacity)
    row = lax.broadcasted_iota(jnp.int32, (capacity, tokens), 0)
    table = jnp.concatenate(
        [(row == place[e : e + 1, :]).astype(f32) for e in range(EXPERTS)], axis=0
    ).astype(bf16)
    width = 512
    for j in range(tokens_ref.shape[1] // width):
        cols = pl.ds(j * width, width)
        part = jnp.dot(table, tokens_ref[:, cols], preferred_element_type=f32).astype(bf16)
        out_ref[:, :, cols] = part.reshape(EXPERTS, capacity, width)


def combine_table_kernel(routes_ref, weight_ref, high_ref, low_ref):
    tokens = routes_ref.shape[1]
    capacity = high_ref.shape[1] // EXPERTS
    routes = routes_ref[...]
    place = slots(routes, tokens, capacity)
    row = lax.broadcasted_iota(jnp.int32, (capacity, tokens), 0)
    parts = []
    for e in range(EXPERTS):
        weight = jnp.where(routes[0:1, :] == e, weight_ref[0:1, :], weight_ref[1:2, :])
        parts.append(jnp.where(row == place[e : e + 1, :], weight, 0.0))
    table = jnp.concatenate(parts, axis=0).T
    high = table.astype(bf16)
    high_ref[...] = high
    low_ref[...] = (table - high.astype(f32)).astype(bf16)


def combine_kernel(high_ref, low_ref, rows_ref, out_ref):
    width = 512
    for j in range(out_ref.shape[1] // width):
        cols = pl.ds(j * width, width)
        rows = rows_ref[:, cols]
        out_ref[:, cols] = (
            jnp.dot(high_ref[...], rows, preferred_element_type=f32)
            + jnp.dot(low_ref[...], rows, preferred_element_type=f32)
        ).astype(bf16)


def ffn_kernel(x_ref, gate_ref, up_ref, down_ref, out_ref, total):
    step = pl.program_id(0)
    x = x_ref[...]
    gate = jnp.dot(x, gate_ref[0], preferred_element_type=f32)
    up = jnp.dot(x, up_ref[0], preferred_element_type=f32)
    hidden = (gate / (1.0 + jnp.exp(-gate)) * up).astype(bf16)
    width = 512
    for j in range(out_ref.shape[1] // width):
        cols = pl.ds(j * width, width)
        part = jnp.dot(hidden, down_ref[0, :, cols], preferred_element_type=f32)

        @pl.when(step == 0)
        def _():
            total[:, cols] = part

        @pl.when(step > 0)
        def _():
            total[:, cols] += part

    @pl.when(step == pl.num_programs(0) - 1)
    def _():
        out_ref[...] = total[...].astype(bf16)


def ffn(x, w_gate, w_up, w_down):
    rows, width = x.shape
    hidden = w_gate.shape[2]
    block = 256
    return pl.pallas_call(
        ffn_kernel,
        grid=(hidden // block,),
        in_specs=[
            pl.BlockSpec((rows, width), lambda i: (0, 0)),
            pl.BlockSpec((1, width, block), lambda i: (0, 0, i)),
            pl.BlockSpec((1, width, block), lambda i: (0, 0, i)),
            pl.BlockSpec((1, block, width), lambda i: (0, i, 0)),
        ],
        out_specs=pl.BlockSpec((rows, width), lambda i: (0, 0)),
        out_shape=jax.ShapeDtypeStruct((rows, width), bf16),
        scratch_shapes=[pltpu.VMEM((rows, width), f32)],
        compiler_params=params(),
        cost_estimate=pl.CostEstimate(
            flops=6 * rows * width * hidden,
            bytes_accessed=6 * width * hidden + 4 * rows * width,
            transcendentals=rows * hidden,
        ),
        name="expert_ffn",
    )(x, w_gate, w_up, w_down)


def split_y_kernel(at_ref, own_ref, got_ref, keep_ref, *send_refs):
    core, me = at_ref[0], at_ref[1]
    width = keep_ref.shape[1]
    half = got_ref.shape[1]
    for k, ref in enumerate((keep_ref,) + send_refs):
        start = jnp.bitwise_xor(me, k) * width
        mine = own_ref[:, pl.ds(pl.multiple_of(core * half + start, width), width)]
        other = got_ref[:, pl.ds(pl.multiple_of(start, width), width)]
        ref[...] = (mine + other).astype(ref.dtype)


def split_z_kernel(at_ref, own_ref, a_ref, b_ref, c_ref, keep_ref, s1_ref, s2_ref, s3_ref, total):
    me = at_ref[2]
    rows, width = keep_ref.shape
    full = (own_ref[...] + a_ref[...].astype(f32)) + (
        b_ref[...].astype(f32) + c_ref[...].astype(f32)
    )
    for p in range(4):
        total[p] = full[(p & 1) * rows : (p & 1) * rows + rows, (p >> 1) * width : (p >> 1) * width + width]
    for k, ref in enumerate((keep_ref, s1_ref, s2_ref, s3_ref)):
        ref[...] = total[jnp.bitwise_xor(me, k)].astype(ref.dtype)


def mean_kernel(replicas, own_ref, a_ref, b_ref, c_ref, mom_ref, out_ref):
    full = (own_ref[...] + a_ref[...].astype(f32)) + (
        b_ref[...].astype(f32) + c_ref[...].astype(f32)
    )
    out_ref[0, 0] = (full * (1.0 / replicas)).astype(bf16)
    out_ref[0, 1] = mom_ref[...].astype(bf16)


def square_kernel(a_ref, b_ref, out_ref):
    total = jnp.zeros(out_ref.shape, f32)
    step = out_ref.shape[0]
    for ref in (a_ref, b_ref):
        for j in range(ref.shape[0]):
            block = ref[j, 0].astype(f32)
            block = block * block
            for i in range(block.shape[0] // step):
                total += block[i * step : i * step + step]
    out_ref[...] = total


def outer_kernel(
    entries, at_ref, s0, s1, s2, s3, near_ref, far_ref, params_ref, local_ref, mom_ref, next_ref, mom_out, scratch
):
    me = at_ref[3]
    squares = (s0[...] + s1[...]) + (s2[...] + s3[...])
    squares = jnp.sum(jnp.sum(squares, axis=1, keepdims=True), axis=0, keepdims=True)
    clip = jnp.minimum(1.0, lax.rsqrt(squares * (1.0 / entries) + clip_epsilon))

    def block(piece, which):
        j = jnp.bitwise_xor(piece, me)
        low = jnp.bitwise_and(j, 15)
        return jnp.where(
            j < 16, near_ref[low, which].astype(f32), far_ref[low, which].astype(f32)
        )

    def piece_of(rep):
        return (rep & 1) * 16 + ((rep >> 1) & 3) * 4 + (rep >> 3)

    for cb in range(16):
        m0 = block(piece_of(2 * cb), 1)
        m1 = block(piece_of(2 * cb + 1), 1)
        for h in range(2):
            rows, cols = pl.ds(h * 48, 48), pl.ds(cb * 128, 128)
            mom = jnp.concatenate([m0[:, h * 64 : h * 64 + 64], m1[:, h * 64 : h * 64 + 64]], axis=1)
            clipped = clip * block(cb * 2 + h, 0)
            after = outer_momentum * mom + clipped
            outer = params_ref[rows, cols] - outer_rate * (outer_momentum * after + clipped)
            local = local_ref[rows, cols].astype(f32)
            next_ref[rows, cols] = (merge_weight * local + (1.0 - merge_weight) * outer).astype(bf16)
    rep = at_ref[4]
    first = jnp.right_shift(rep, 1) * 2
    scratch[...] = jnp.zeros_like(scratch)
    scratch[0:48, :] = block(first, 0)
    scratch[48:96, :] = block(first + 1, 0)
    scratch[...] = scratch[...].T
    start = pl.multiple_of(jnp.bitwise_and(rep, 1) * 64, 64)
    mom_out[...] = outer_momentum * mom_ref[...] + clip * scratch[pl.ds(start, 64), 0:96]


def smem():
    return pl.BlockSpec(memory_space=pltpu.SMEM)


def swap(value, axis, bits):
    size = lax.axis_size(axis)
    return lax.ppermute(value, axis, [(i, i ^ bits) for i in range(size)])


def outer_step(pseudo_grad, global_params, momentum, local_params):
    own = pseudo_grad[0]
    rows, width = own.shape
    core, y, zh = lax.axis_index("c"), lax.axis_index("y"), lax.axis_index("zh")
    rep = (zh * 4 + y) * 2 + core
    at = jnp.stack([core, y, zh, core * 16 + y * 4 + zh, rep]).astype(jnp.int32)
    half = width // 2
    other = lax.dynamic_slice_in_dim(own, (1 - core) * half, half, 1)
    got = swap(other, "c", 1)
    quarter = half // 4
    keep, *sends = pl.pallas_call(
        split_y_kernel,
        in_specs=[smem()] + whole(2),
        out_specs=whole(4),
        out_shape=[jax.ShapeDtypeStruct((rows, quarter), f32)]
        + [jax.ShapeDtypeStruct((rows, quarter), bf16)] * 3,
        compiler_params=params(),
        name="delta_split_y",
    )(at, own, got)
    got = [swap(s, "y", k + 1) for k, s in enumerate(sends)]
    keep, *sends = pl.pallas_call(
        split_z_kernel,
        in_specs=[smem()] + whole(4),
        out_specs=whole(4),
        out_shape=[jax.ShapeDtypeStruct((rows // 2, quarter // 2), f32)] * 4,
        scratch_shapes=[pltpu.VMEM((4, rows // 2, quarter // 2), f32)],
        compiler_params=params(),
        name="delta_split_z",
    )(at, keep, *got)
    got = [swap(s, "zh", k + 1) for k, s in enumerate(sends)]
    mom_block = jnp.concatenate([momentum[: rows // 2], momentum[rows // 2 :]], axis=1)
    block = pl.pallas_call(
        lambda *refs: mean_kernel(32, *refs),
        in_specs=whole(5),
        out_specs=whole(1)[0],
        out_shape=jax.ShapeDtypeStruct((1, 2, rows // 2, quarter // 2), bf16),
        compiler_params=params(),
        name="delta_mean",
    )(keep, *got, mom_block)
    block = jnp.concatenate([block] + [swap(block, "zh", k) for k in (1, 2, 3)], axis=0)
    block = jnp.concatenate([block] + [swap(block, "y", k) for k in (1, 2, 3)], axis=0)
    far = swap(block, "c", 1)
    squares = pl.pallas_call(
        square_kernel,
        in_specs=whole(2),
        out_specs=whole(1)[0],
        out_shape=jax.ShapeDtypeStruct((8, 128), f32),
        compiler_params=params(),
        name="delta_squares",
    )(block, far)
    squares = squares + swap(squares, "zl", 1)
    parts = [squares] + [swap(squares, "x", k) for k in (1, 2, 3)]
    entries = float(rows * 8 * width)
    local_next, momentum_next = pl.pallas_call(
        lambda *refs: outer_kernel(entries, *refs),
        in_specs=[smem()] + whole(9),
        out_specs=whole(2),
        out_shape=[
            jax.ShapeDtypeStruct((rows, width), bf16),
            jax.ShapeDtypeStruct((momentum.shape[1], rows), f32),
        ],
        scratch_shapes=[pltpu.VMEM((128, 128), f32)],
        compiler_params=params(),
        name="outer_update",
    )(at, *parts, block, far, global_params, local_params[0], momentum.T)
    return momentum_next.T, local_next[None]


def local(
    tokens, routes, route_weight, w_gate, w_up, w_down, pseudo_grad, global_params, momentum, local_params
):
    tok_rows, feat_width = tokens.shape
    capacity = tok_rows * 3 // 8
    routes_t, weight_t = routes.T, route_weight.T
    outgoing = pl.pallas_call(
        dispatch_kernel,
        in_specs=whole(2),
        out_specs=whole(1)[0],
        out_shape=jax.ShapeDtypeStruct((EXPERTS, capacity, feat_width), bf16),
        compiler_params=params(),
        name="dispatch",
    )(routes_t, tokens)
    high, low = pl.pallas_call(
        combine_table_kernel,
        in_specs=whole(2),
        out_specs=whole(2),
        out_shape=[jax.ShapeDtypeStruct((tok_rows, EXPERTS * capacity), bf16)] * 2,
        compiler_params=params(),
        name="combine_table",
    )(routes_t, weight_t)
    received = lax.all_to_all(outgoing, SHARD, split_axis=0, concat_axis=0, tiled=True)
    result = ffn(received.reshape(EXPERTS * capacity, feat_width), w_gate, w_up, w_down)
    result = result.reshape(EXPERTS, capacity, feat_width)
    returned = lax.all_to_all(result, SHARD, split_axis=0, concat_axis=0, tiled=True)
    moe_out = pl.pallas_call(
        combine_kernel,
        in_specs=whole(3),
        out_specs=whole(1)[0],
        out_shape=jax.ShapeDtypeStruct((tok_rows, feat_width), bf16),
        compiler_params=params(),
        name="combine",
    )(high, low, returned.reshape(EXPERTS * capacity, feat_width))
    momentum_next, local_next = outer_step(pseudo_grad, global_params, momentum, local_params)
    return (moe_out, momentum_next, local_next)


def solution(mesh):
    fine = Mesh(mesh.devices.reshape(4, 4, 2, 4, 2), REP + SHARD)
    in_specs = (
        P(REP + SHARD, None),
        P(REP + SHARD, None),
        P(REP + SHARD, None),
        P(SHARD, None, None),
        P(SHARD, None, None),
        P(SHARD, None, None),
        P(REP, SHARD, None),
        P(SHARD, None),
        P(SHARD, REP),
        P(REP, SHARD, None),
    )
    out_specs = (P(REP + SHARD, None), P(SHARD, REP), P(REP, SHARD, None))
    return jax.shard_map(local, mesh=fine, in_specs=in_specs, out_specs=out_specs, check_vma=False)
```

```python
import jax
import jax.numpy as jnp
from jax import lax
from jax.experimental import pallas as pl
from jax.experimental.pallas import tpu as pltpu
from jax.sharding import Mesh
from jax.sharding import PartitionSpec as P

f32 = jnp.float32
bf16 = jnp.bfloat16

outer_momentum = 0.9
outer_rate = 0.7
merge_weight = 0.5
clip_epsilon = 1e-06

EXPERTS = 8
REP = ("zh", "y", "c")
SHARD = ("x", "zl")
VMEM_LIMIT = 16 * 1024 * 1024


def params(**more):
    return pltpu.CompilerParams(vmem_limit_bytes=VMEM_LIMIT, **more)


def whole(count):
    return [pl.BlockSpec(memory_space=pltpu.VMEM)] * count


def slots(routes, tokens, capacity):
    ids = lax.broadcasted_iota(jnp.int32, (EXPERTS, tokens), 0)
    named = jnp.logical_or(routes[0:1, :] == ids, routes[1:2, :] == ids)
    before = lax.broadcasted_iota(jnp.int32, (tokens, tokens), 0) < lax.broadcasted_iota(
        jnp.int32, (tokens, tokens), 1
    )
    place = jnp.dot(
        named.astype(f32).astype(bf16), before.astype(f32).astype(bf16), preferred_element_type=f32
    )
    return jnp.where(named, place.astype(jnp.int32), capacity)


def dispatch_kernel(routes_ref, tokens_ref, out_ref):
    tokens = tokens_ref.shape[0]
    capacity = out_ref.shape[1]
    place = slots(routes_ref[...], tokens, capacity)
    row = lax.broadcasted_iota(jnp.int32, (capacity, tokens), 0)
    table = jnp.concatenate(
        [(row == place[e : e + 1, :]).astype(f32) for e in range(EXPERTS)], axis=0
    ).astype(bf16)
    width = 512
    for j in range(tokens_ref.shape[1] // width):
        cols = pl.ds(j * width, width)
        part = jnp.dot(table, tokens_ref[:, cols], preferred_element_type=f32).astype(bf16)
        out_ref[:, :, cols] = part.reshape(EXPERTS, capacity, width)


def combine_table_kernel(routes_ref, weight_ref, high_ref, low_ref):
    tokens = routes_ref.shape[1]
    capacity = high_ref.shape[1] // EXPERTS
    routes = routes_ref[...]
    place = slots(routes, tokens, capacity)
    row = lax.broadcasted_iota(jnp.int32, (capacity, tokens), 0)
    parts = []
    for e in range(EXPERTS):
        weight = jnp.where(routes[0:1, :] == e, weight_ref[0:1, :], weight_ref[1:2, :])
        parts.append(jnp.where(row == place[e : e + 1, :], weight, 0.0))
    table = jnp.concatenate(parts, axis=0).T
    high = table.astype(bf16)
    high_ref[...] = high
    low_ref[...] = (table - high.astype(f32)).astype(bf16)


def combine_kernel(high_ref, low_ref, rows_ref, out_ref):
    width = 512
    for j in range(out_ref.shape[1] // width):
        cols = pl.ds(j * width, width)
        rows = rows_ref[:, cols]
        out_ref[:, cols] = (
            jnp.dot(high_ref[...], rows, preferred_element_type=f32)
            + jnp.dot(low_ref[...], rows, preferred_element_type=f32)
        ).astype(bf16)


def ffn_kernel(
    x_hbm, gate_hbm, up_hbm, down_hbm, out_hbm, x_ref, gate_ref, up_ref, down_ref, hidden_ref, out_ref, sems
):
    block, wide = 256, 512
    count, last = hidden_ref.shape[1] // block, out_ref.shape[1] // wide
    copies = [pltpu.make_async_copy(x_hbm, x_ref, sems.at[0])]
    for i in range(count):
        cols = pl.ds(i * block, block)
        for hbm, ref in ((gate_hbm, gate_ref), (up_hbm, up_ref)):
            copies.append(
                pltpu.make_async_copy(hbm.at[0, :, cols], ref.at[:, cols], sems.at[len(copies)])
            )
    for i in range(last):
        cols = pl.ds(i * wide, wide)
        copies.append(
            pltpu.make_async_copy(down_hbm.at[0, :, cols], down_ref.at[:, cols], sems.at[len(copies)])
        )
    for copy in copies:
        copy.start()
    copies[0].wait()
    for i in range(count):
        cols = pl.ds(i * block, block)
        copies[2 * i + 1].wait()
        gate = jnp.dot(x_ref[...], gate_ref[:, cols], preferred_element_type=f32)
        copies[2 * i + 2].wait()
        up = jnp.dot(x_ref[...], up_ref[:, cols], preferred_element_type=f32)
        hidden_ref[:, cols] = (gate / (1.0 + jnp.exp(-gate)) * up).astype(bf16)
    results = []
    for i in range(last):
        cols = pl.ds(i * wide, wide)
        copies[2 * count + 1 + i].wait()
        out_ref[:, cols] = jnp.dot(
            hidden_ref[...], down_ref[:, cols], preferred_element_type=f32
        ).astype(bf16)
        results.append(
            pltpu.make_async_copy(out_ref.at[:, cols], out_hbm.at[:, cols], sems.at[len(copies) + i])
        )
        results[-1].start()
    for copy in results:
        copy.wait()


def ffn(x, w_gate, w_up, w_down):
    rows, width = x.shape
    hidden = w_gate.shape[2]
    anywhere = pl.BlockSpec(memory_space=pl.ANY)
    return pl.pallas_call(
        ffn_kernel,
        in_specs=[anywhere] * 4,
        out_specs=anywhere,
        out_shape=jax.ShapeDtypeStruct((rows, width), bf16),
        scratch_shapes=[
            pltpu.VMEM((rows, width), bf16),
            pltpu.VMEM((width, hidden), bf16),
            pltpu.VMEM((width, hidden), bf16),
            pltpu.VMEM((hidden, width), bf16),
            pltpu.VMEM((rows, hidden), bf16),
            pltpu.VMEM((rows, width), bf16),
            pltpu.SemaphoreType.DMA((1 + hidden // 128 + width // 256,)),
        ],
        compiler_params=pltpu.CompilerParams(vmem_limit_bytes=58 * 1024 * 1024),
        cost_estimate=pl.CostEstimate(
            flops=6 * rows * width * hidden,
            bytes_accessed=6 * width * hidden + 4 * rows * width,
            transcendentals=rows * hidden,
        ),
        name="expert_ffn",
    )(x, w_gate, w_up, w_down)


def halve_first_kernel(at_ref, own_ref, got_ref, keep_ref, send_ref):
    core, bit = at_ref[0], at_ref[1]
    half, width = got_ref.shape[1], keep_ref.shape[1]
    for ref, which in ((send_ref, 1 - bit), (keep_ref, bit)):
        mine = own_ref[0, :, pl.ds(pl.multiple_of(core * half + which * width, width), width)]
        other = got_ref[:, pl.ds(pl.multiple_of(which * width, width), width)]
        ref[...] = (mine + other).astype(ref.dtype)


def halve_kernel(at_ref, own_ref, got_ref, keep_ref, send_ref):
    bit, width = at_ref[2], keep_ref.shape[1]
    for ref, which in ((send_ref, 1 - bit), (keep_ref, bit)):
        cols = pl.ds(pl.multiple_of(which * width, width), width)
        ref[...] = (own_ref[:, cols] + got_ref[:, cols].astype(f32)).astype(ref.dtype)


def add_z_first_kernel(own_ref, got_ref, mom_ref, keep_ref, send_ref):
    rows = send_ref.shape[1]
    total = own_ref[...] + got_ref[...].astype(f32)
    for p in range(4):
        keep_ref[p] = total[(p & 1) * rows : (p & 1) * rows + rows, (p >> 1) * 128 : (p >> 1) * 128 + 128]
    send_ref[0:4] = keep_ref[...].astype(bf16)
    send_ref[4] = mom_ref[...].astype(bf16)


def add_z_kernel(own_ref, sent_ref, got_ref, keep_ref, send_ref):
    total = own_ref[...] + got_ref[0:4].astype(f32)
    keep_ref[...] = total
    send_ref[0:4] = total.astype(bf16)
    send_ref[4] = sent_ref[4]
    send_ref[5] = got_ref[4]


def mean_kernel(replicas, own_ref, sent_ref, got_ref, out_ref):
    total = own_ref[...] + got_ref[0:4].astype(f32)
    out_ref[0, 0:4] = (total * (1.0 / replicas)).astype(bf16)
    out_ref[0, 4:6] = sent_ref[4:6]
    out_ref[0, 6:8] = got_ref[4:6]


def square_kernel(a_ref, b_ref, out_ref):
    total = jnp.zeros(out_ref.shape, f32)
    step = out_ref.shape[0]
    for ref in (a_ref, b_ref):
        for j in range(4):
            for k in range(4):
                block = ref[j, k].astype(f32)
                block = block * block
                for i in range(block.shape[0] // step):
                    total += block[i * step : i * step + step]
    out_ref[...] = total


def quarter_of(y):
    return ((y & 1) ^ (y >> 1)) * 2 + (y >> 1)


def outer_kernel(entries, at_ref, near_s, far_s, near_ref, far_ref, params_ref, local_ref, mom_ref, next_ref, mom_out, scratch):
    core, quarter, zh, rep = at_ref[0], at_ref[3], at_ref[4], at_ref[5]
    squares = near_s[...] + far_s[...]
    squares = jnp.sum(jnp.sum(squares, axis=1, keepdims=True), axis=0, keepdims=True)
    clip = jnp.minimum(1.0, lax.rsqrt(squares * (1.0 / entries) + clip_epsilon))

    def delta(side, piece, slot):
        j = jnp.bitwise_xor(piece, quarter)
        return jnp.where(
            core == side, near_ref[j, slot].astype(f32), far_ref[j, slot].astype(f32)
        )

    for cb in range(16):
        j = jnp.bitwise_xor(quarter_of(cb & 3), quarter)
        apart = jnp.bitwise_xor(zh, cb >> 2)
        high = jnp.right_shift(apart, 1)
        slot = 4 + high * 2 + jnp.bitwise_xor(jnp.bitwise_and(apart, 1), high)
        near, far = near_ref[j, slot].astype(f32), far_ref[j, slot].astype(f32)
        m0, m1 = jnp.where(core == 0, near, far), jnp.where(core == 0, far, near)
        for h in range(2):
            rows, cols = pl.ds(h * 48, 48), pl.ds(cb * 128, 128)
            mom = jnp.concatenate([m0[:, h * 64 : h * 64 + 64], m1[:, h * 64 : h * 64 + 64]], axis=1)
            clipped = clip * delta(cb >> 3, (cb >> 1) & 3, (cb & 1) * 2 + h)
            after = outer_momentum * mom + clipped
            outer = params_ref[rows, cols] - outer_rate * (outer_momentum * after + clipped)
            local = local_ref[0, rows, cols].astype(f32)
            next_ref[0, rows, cols] = (merge_weight * local + (1.0 - merge_weight) * outer).astype(bf16)
    cb = jnp.right_shift(rep, 1)
    side, piece = jnp.right_shift(cb, 3), jnp.bitwise_and(jnp.right_shift(cb, 1), 3)
    scratch[...] = jnp.zeros_like(scratch)
    for h in range(2):
        scratch[h * 48 : h * 48 + 48, :] = delta(side, piece, jnp.bitwise_and(cb, 1) * 2 + h)
    scratch[...] = scratch[...].T
    start = pl.multiple_of(core * 64, 64)
    mom_out[...] = outer_momentum * mom_ref[...] + clip * scratch[pl.ds(start, 64), 0:96]


def smem():
    return pl.BlockSpec(memory_space=pltpu.SMEM)


def swap(value, axis, bits):
    size = lax.axis_size(axis)
    return lax.ppermute(value, axis, [(i, i ^ bits) for i in range(size)])


def outer_sum(pseudo_grad, momentum):
    rows, width = pseudo_grad.shape[1:]
    core, y, zh = lax.axis_index("c"), lax.axis_index("y"), lax.axis_index("zh")
    rep = (zh * 4 + y) * 2 + core
    first, second = (y & 1) ^ (y >> 1), y >> 1
    at = jnp.stack([core, first, second, first * 2 + second, zh, rep]).astype(jnp.int32)
    half = width // 2
    got = swap(lax.dynamic_slice_in_dim(pseudo_grad[0], (1 - core) * half, half, 1), "c", 1)
    keep, send = pl.pallas_call(
        halve_first_kernel,
        in_specs=[smem()] + whole(2),
        out_specs=whole(2),
        out_shape=[jax.ShapeDtypeStruct((rows, half // 2), t) for t in (f32, bf16)],
        compiler_params=params(),
        name="delta_halve_first",
    )(at, pseudo_grad, got)
    got = swap(send, "y", 1)
    keep, send = pl.pallas_call(
        halve_kernel,
        in_specs=[smem()] + whole(2),
        out_specs=whole(2),
        out_shape=[jax.ShapeDtypeStruct((rows, half // 4), t) for t in (f32, bf16)],
        compiler_params=params(),
        name="delta_halve",
    )(at, keep, got)
    got = swap(send, "y", 3)
    part = (rows // 2, half // 8)
    mom_block = jnp.concatenate([momentum[: rows // 2], momentum[rows // 2 :]], axis=1)
    keep, send = pl.pallas_call(
        add_z_first_kernel,
        in_specs=whole(3),
        out_specs=whole(2),
        out_shape=[jax.ShapeDtypeStruct((4,) + part, f32), jax.ShapeDtypeStruct((5,) + part, bf16)],
        compiler_params=params(),
        name="delta_add_z_first",
    )(keep, got, mom_block)
    got = swap(send, "zh", 1)
    keep, send = pl.pallas_call(
        add_z_kernel,
        in_specs=whole(3),
        out_specs=whole(2),
        out_shape=[jax.ShapeDtypeStruct((4,) + part, f32), jax.ShapeDtypeStruct((6,) + part, bf16)],
        compiler_params=params(),
        name="delta_add_z",
    )(keep, send, got)
    got = swap(send, "zh", 3)
    block = pl.pallas_call(
        lambda *refs: mean_kernel(32, *refs),
        in_specs=whole(3),
        out_specs=whole(1)[0],
        out_shape=jax.ShapeDtypeStruct((1, 8) + part, bf16),
        compiler_params=params(),
        name="delta_mean",
    )(keep, send, got)
    return at, block


def outer_finish(at, block, global_params, momentum, local_params):
    rows, width = global_params.shape
    block = jnp.concatenate([block, swap(block, "y", 3)], axis=0)
    block = jnp.concatenate([block, swap(block, "y", 1)], axis=0)
    far = swap(block, "c", 1)
    squares = pl.pallas_call(
        square_kernel,
        in_specs=whole(2),
        out_specs=whole(1)[0],
        out_shape=jax.ShapeDtypeStruct((8, 128), f32),
        compiler_params=params(),
        name="delta_squares",
    )(block, far)
    squares = squares + swap(squares, "zl", 1)
    squares = squares + swap(squares, "x", 1)
    entries = float(rows * 8 * width)
    local_next, momentum_next = pl.pallas_call(
        lambda *refs: outer_kernel(entries, *refs),
        in_specs=[smem()] + whole(7),
        out_specs=whole(2),
        out_shape=[
            jax.ShapeDtypeStruct((1, rows, width), bf16),
            jax.ShapeDtypeStruct((momentum.shape[1], rows), f32),
        ],
        scratch_shapes=[pltpu.VMEM((128, 128), f32)],
        compiler_params=params(),
        name="outer_update",
    )(at, squares, swap(squares, "x", 3), block, far, global_params, local_params, momentum.T)
    return momentum_next.T, local_next


def local(
    tokens, routes, route_weight, w_gate, w_up, w_down, pseudo_grad, global_params, momentum, local_params
):
    tok_rows, feat_width = tokens.shape
    capacity = tok_rows * 3 // 8
    routes_t, weight_t = routes.T, route_weight.T
    outgoing = pl.pallas_call(
        dispatch_kernel,
        in_specs=whole(2),
        out_specs=whole(1)[0],
        out_shape=jax.ShapeDtypeStruct((EXPERTS, capacity, feat_width), bf16),
        compiler_params=params(),
        name="dispatch",
    )(routes_t, tokens)
    high, low = pl.pallas_call(
        combine_table_kernel,
        in_specs=whole(2),
        out_specs=whole(2),
        out_shape=[jax.ShapeDtypeStruct((tok_rows, EXPERTS * capacity), bf16)] * 2,
        compiler_params=params(),
        name="combine_table",
    )(routes_t, weight_t)
    at, block = outer_sum(pseudo_grad, momentum)
    received = lax.all_to_all(outgoing, SHARD, split_axis=0, concat_axis=0, tiled=True)
    received, block = lax.optimization_barrier((received, block))
    result = ffn(received.reshape(EXPERTS * capacity, feat_width), w_gate, w_up, w_down)
    result = result.reshape(EXPERTS, capacity, feat_width)
    returned = lax.all_to_all(result, SHARD, split_axis=0, concat_axis=0, tiled=True)
    moe_out = pl.pallas_call(
        combine_kernel,
        in_specs=whole(3),
        out_specs=whole(1)[0],
        out_shape=jax.ShapeDtypeStruct((tok_rows, feat_width), bf16),
        compiler_params=params(),
        name="combine",
    )(high, low, returned.reshape(EXPERTS * capacity, feat_width))
    momentum_next, local_next = outer_finish(at, block, global_params, momentum, local_params)
    return (moe_out, momentum_next, local_next)


def solution(mesh):
    fine = Mesh(mesh.devices.reshape(4, 4, 2, 4, 2), REP + SHARD)
    in_specs = (
        P(REP + SHARD, None),
        P(REP + SHARD, None),
        P(REP + SHARD, None),
        P(SHARD, None, None),
        P(SHARD, None, None),
        P(SHARD, None, None),
        P(REP, SHARD, None),
        P(SHARD, None),
        P(SHARD, REP),
        P(REP, SHARD, None),
    )
    out_specs = (P(REP + SHARD, None), P(SHARD, REP), P(REP, SHARD, None))
    return jax.shard_map(local, mesh=fine, in_specs=in_specs, out_specs=out_specs, check_vma=False)
```

```python
import jax
import jax.numpy as jnp
from jax import lax
from jax.experimental import pallas as pl
from jax.experimental.pallas import tpu as pltpu
from jax.sharding import Mesh
from jax.sharding import PartitionSpec as P

f32 = jnp.float32
bf16 = jnp.bfloat16

outer_momentum = 0.9
outer_rate = 0.7
merge_weight = 0.5
clip_epsilon = 1e-06

EXPERTS = 8
REP = ("zh", "y", "c")
SHARD = ("x", "zl")
VMEM_LIMIT = 8 * 1024 * 1024
FFN_LIMIT = 52 * 1000000
DISPATCH_LIMIT = 58 * 1024 * 1024


def params(**more):
    return pltpu.CompilerParams(vmem_limit_bytes=VMEM_LIMIT, **more)


def whole(count):
    return [pl.BlockSpec(memory_space=pltpu.VMEM)] * count


def slots(routes, tokens, capacity):
    ids = lax.broadcasted_iota(jnp.int32, (EXPERTS, tokens), 0)
    named = jnp.logical_or(routes[0:1, :] == ids, routes[1:2, :] == ids)
    before = lax.broadcasted_iota(jnp.int32, (tokens, tokens), 0) < lax.broadcasted_iota(
        jnp.int32, (tokens, tokens), 1
    )
    place = jnp.dot(
        named.astype(f32).astype(bf16), before.astype(f32).astype(bf16), preferred_element_type=f32
    )
    return jnp.where(named, place.astype(jnp.int32), capacity)


def dispatch_kernel(routes_hbm, tokens_hbm, out_hbm, routes_ref, tokens_ref, out_ref, sems):
    tokens = tokens_ref.shape[0]
    capacity = out_ref.shape[1]
    width = 512
    parts = [pl.ds(j * width, width) for j in range(tokens_ref.shape[1] // width)]
    first = pltpu.make_async_copy(routes_hbm, routes_ref, sems.at[0])
    first.start()
    reads = [
        pltpu.make_async_copy(tokens_hbm.at[:, cols], tokens_ref.at[:, cols], sems.at[1 + j])
        for j, cols in enumerate(parts)
    ]
    for copy in reads:
        copy.start()
    first.wait()
    place = slots(routes_ref[...], tokens, capacity)
    row = lax.broadcasted_iota(jnp.int32, (capacity, tokens), 0)
    table = jnp.concatenate(
        [(row == place[e : e + 1, :]).astype(f32) for e in range(EXPERTS)], axis=0
    ).astype(bf16)
    writes = []
    for j, cols in enumerate(parts):
        reads[j].wait()
        part = jnp.dot(table, tokens_ref[:, cols], preferred_element_type=f32).astype(bf16)
        out_ref[:, :, cols] = part.reshape(EXPERTS, capacity, width)
        writes.append(
            pltpu.make_async_copy(out_ref.at[:, :, cols], out_hbm.at[:, :, cols], sems.at[1 + len(parts) + j])
        )
        writes[-1].start()
    for copy in writes:
        copy.wait()


def combine_kernel(routes_ref, weight_ref, rows_ref, out_ref):
    tokens = routes_ref.shape[1]
    capacity = rows_ref.shape[0] // EXPERTS
    routes = routes_ref[...]
    place = slots(routes, tokens, capacity)
    row = lax.broadcasted_iota(jnp.int32, (capacity, tokens), 0)
    parts = []
    for e in range(EXPERTS):
        weight = jnp.where(routes[0:1, :] == e, weight_ref[0:1, :], weight_ref[1:2, :])
        parts.append(jnp.where(row == place[e : e + 1, :], weight, 0.0))
    table = jnp.concatenate(parts, axis=0).T
    high = table.astype(bf16)
    low = (table - high.astype(f32)).astype(bf16)
    width = 512
    for j in range(out_ref.shape[1] // width):
        cols = pl.ds(j * width, width)
        rows = rows_ref[:, cols]
        out_ref[:, cols] = (
            jnp.dot(high, rows, preferred_element_type=f32)
            + jnp.dot(low, rows, preferred_element_type=f32)
        ).astype(bf16)


def ffn_kernel(
    x_ref, gate_hbm, up_hbm, down_hbm, out_hbm, gate_ref, up_ref, down_ref, gated_ref, hidden_ref, out_ref, sems
):
    block, wide = 256, 512
    width, hidden = gate_ref.shape
    half, count = width // 2, hidden // block
    copies = []
    for hbm, ref in ((gate_hbm, gate_ref), (up_hbm, up_ref)):
        for i in range(2):
            rows = pl.ds(i * half, half)
            copies.append(pltpu.make_async_copy(hbm.at[0, rows], ref.at[rows], sems.at[len(copies)]))
    copies.append(pltpu.make_async_copy(down_hbm.at[0], down_ref, sems.at[4]))
    for copy in copies:
        copy.start()
    for i in range(2):
        rows = pl.ds(i * half, half)
        copies[i].wait()
        for n in range(count):
            cols = pl.ds(n * block, block)
            part = jnp.dot(x_ref[:, rows], gate_ref[rows, cols], preferred_element_type=f32)
            gated_ref[:, cols] = part if i == 0 else gated_ref[:, cols] + part
    copies[2].wait()
    copies[3].wait()
    for n in range(count):
        cols = pl.ds(n * block, block)
        up = jnp.dot(x_ref[...], up_ref[:, cols], preferred_element_type=f32)
        gate = gated_ref[:, cols]
        hidden_ref[:, cols] = (gate / (1.0 + jnp.exp(-gate)) * up).astype(bf16)
    copies[4].wait()
    results = []
    for n in range(width // wide):
        cols = pl.ds(n * wide, wide)
        out_ref[:, cols] = jnp.dot(
            hidden_ref[...], down_ref[:, cols], preferred_element_type=f32
        ).astype(bf16)
        results.append(pltpu.make_async_copy(out_ref.at[:, cols], out_hbm.at[:, cols], sems.at[5 + n]))
        results[-1].start()
    for copy in results:
        copy.wait()


def ffn(x, w_gate, w_up, w_down):
    rows, width = x.shape
    hidden = w_gate.shape[2]
    anywhere = pl.BlockSpec(memory_space=pl.ANY)
    return pl.pallas_call(
        ffn_kernel,
        in_specs=whole(1) + [anywhere] * 3,
        out_specs=anywhere,
        out_shape=jax.ShapeDtypeStruct((rows, width), bf16),
        scratch_shapes=[
            pltpu.VMEM((width, hidden), bf16),
            pltpu.VMEM((width, hidden), bf16),
            pltpu.VMEM((hidden, width), bf16),
            pltpu.VMEM((rows, hidden), f32),
            pltpu.VMEM((rows, hidden), bf16),
            pltpu.VMEM((rows, width), bf16),
            pltpu.SemaphoreType.DMA((5 + width // 512,)),
        ],
        compiler_params=pltpu.CompilerParams(vmem_limit_bytes=FFN_LIMIT),
        cost_estimate=pl.CostEstimate(
            flops=6 * rows * width * hidden,
            bytes_accessed=6 * width * hidden + 4 * rows * width,
            transcendentals=rows * hidden,
        ),
        name="expert_ffn",
    )(x, w_gate, w_up, w_down)


def halve_first_kernel(at_ref, own_ref, got_ref, keep_ref, send_ref):
    core, bit = at_ref[0], at_ref[1]
    half, width = got_ref.shape[1], keep_ref.shape[1]
    for ref, which in ((send_ref, 1 - bit), (keep_ref, bit)):
        mine = own_ref[0, :, pl.ds(pl.multiple_of(core * half + which * width, width), width)]
        other = got_ref[:, pl.ds(pl.multiple_of(which * width, width), width)]
        ref[...] = (mine + other).astype(ref.dtype)


def halve_kernel(at_ref, own_ref, got_ref, keep_ref, send_ref):
    bit, width = at_ref[2], keep_ref.shape[1]
    for ref, which in ((send_ref, 1 - bit), (keep_ref, bit)):
        cols = pl.ds(pl.multiple_of(which * width, width), width)
        ref[...] = (own_ref[:, cols] + got_ref[:, cols].astype(f32)).astype(ref.dtype)


def add_z_first_kernel(own_ref, got_ref, mom_ref, keep_ref, send_ref):
    rows = send_ref.shape[1]
    total = own_ref[...] + got_ref[...].astype(f32)
    for p in range(4):
        keep_ref[p] = total[(p & 1) * rows : (p & 1) * rows + rows, (p >> 1) * 128 : (p >> 1) * 128 + 128]
    send_ref[0:4] = keep_ref[...].astype(bf16)
    send_ref[4] = mom_ref[...].astype(bf16)


def add_z_kernel(own_ref, sent_ref, got_ref, keep_ref, send_ref):
    total = own_ref[...] + got_ref[0:4].astype(f32)
    keep_ref[...] = total
    send_ref[0:4] = total.astype(bf16)
    send_ref[4] = sent_ref[4]
    send_ref[5] = got_ref[4]


def mean_kernel(replicas, own_ref, sent_ref, got_ref, out_ref):
    total = own_ref[...] + got_ref[0:4].astype(f32)
    out_ref[0, 0:4] = (total * (1.0 / replicas)).astype(bf16)
    out_ref[0, 4:6] = sent_ref[4:6]
    out_ref[0, 6:8] = got_ref[4:6]


def square_kernel(a_ref, b_ref, out_ref):
    total = jnp.zeros(out_ref.shape, f32)
    step = out_ref.shape[0]
    for ref in (a_ref, b_ref):
        for j in range(4):
            for k in range(4):
                block = ref[j, k].astype(f32)
                block = block * block
                for i in range(block.shape[0] // step):
                    total += block[i * step : i * step + step]
    out_ref[...] = total


def quarter_of(y):
    return ((y & 1) ^ (y >> 1)) * 2 + (y >> 1)


def outer_kernel(entries, at_ref, near_s, far_s, near_ref, far_ref, params_ref, local_ref, mom_ref, next_ref, mom_out, scratch):
    core, quarter, zh, rep = at_ref[0], at_ref[3], at_ref[4], at_ref[5]
    squares = near_s[...] + far_s[...]
    squares = jnp.sum(jnp.sum(squares, axis=1, keepdims=True), axis=0, keepdims=True)
    clip = jnp.minimum(1.0, lax.rsqrt(squares * (1.0 / entries) + clip_epsilon))

    def delta(side, piece, slot):
        j = jnp.bitwise_xor(piece, quarter)
        return jnp.where(
            core == side, near_ref[j, slot].astype(f32), far_ref[j, slot].astype(f32)
        )

    for cb in range(16):
        j = jnp.bitwise_xor(quarter_of(cb & 3), quarter)
        apart = jnp.bitwise_xor(zh, cb >> 2)
        high = jnp.right_shift(apart, 1)
        slot = 4 + high * 2 + jnp.bitwise_xor(jnp.bitwise_and(apart, 1), high)
        near, far = near_ref[j, slot].astype(f32), far_ref[j, slot].astype(f32)
        m0, m1 = jnp.where(core == 0, near, far), jnp.where(core == 0, far, near)
        for h in range(2):
            rows, cols = pl.ds(h * 48, 48), pl.ds(cb * 128, 128)
            mom = jnp.concatenate([m0[:, h * 64 : h * 64 + 64], m1[:, h * 64 : h * 64 + 64]], axis=1)
            clipped = clip * delta(cb >> 3, (cb >> 1) & 3, (cb & 1) * 2 + h)
            after = outer_momentum * mom + clipped
            outer = params_ref[rows, cols] - outer_rate * (outer_momentum * after + clipped)
            local = local_ref[0, rows, cols].astype(f32)
            next_ref[0, rows, cols] = (merge_weight * local + (1.0 - merge_weight) * outer).astype(bf16)
    cb = jnp.right_shift(rep, 1)
    side, piece = jnp.right_shift(cb, 3), jnp.bitwise_and(jnp.right_shift(cb, 1), 3)
    scratch[...] = jnp.zeros_like(scratch)
    for h in range(2):
        scratch[h * 48 : h * 48 + 48, :] = delta(side, piece, jnp.bitwise_and(cb, 1) * 2 + h)
    scratch[...] = scratch[...].T
    start = pl.multiple_of(core * 64, 64)
    mom_out[...] = outer_momentum * mom_ref[...] + clip * scratch[pl.ds(start, 64), 0:96]


def smem():
    return pl.BlockSpec(memory_space=pltpu.SMEM)


def swap(value, axis, bits):
    size = lax.axis_size(axis)
    return lax.ppermute(value, axis, [(i, i ^ bits) for i in range(size)])


def outer_sum(pseudo_grad, momentum, outgoing):
    rows, width = pseudo_grad.shape[1:]
    core, y, zh = lax.axis_index("c"), lax.axis_index("y"), lax.axis_index("zh")
    rep = (zh * 4 + y) * 2 + core
    first, second = (y & 1) ^ (y >> 1), y >> 1
    at = jnp.stack([core, first, second, first * 2 + second, zh, rep]).astype(jnp.int32)
    half = width // 2
    got = swap(lax.dynamic_slice_in_dim(pseudo_grad[0], (1 - core) * half, half, 1), "c", 1)
    keep, send = pl.pallas_call(
        halve_first_kernel,
        in_specs=[smem()] + whole(2),
        out_specs=whole(2),
        out_shape=[jax.ShapeDtypeStruct((rows, half // 2), t) for t in (f32, bf16)],
        compiler_params=params(),
        name="delta_halve_first",
    )(at, pseudo_grad, got)
    outgoing, keep, send = lax.optimization_barrier((outgoing, keep, send))
    got = swap(send, "y", 1)
    keep, send = pl.pallas_call(
        halve_kernel,
        in_specs=[smem()] + whole(2),
        out_specs=whole(2),
        out_shape=[jax.ShapeDtypeStruct((rows, half // 4), t) for t in (f32, bf16)],
        compiler_params=params(),
        name="delta_halve",
    )(at, keep, got)
    got = swap(send, "y", 3)
    part = (rows // 2, half // 8)
    mom_block = jnp.concatenate([momentum[: rows // 2], momentum[rows // 2 :]], axis=1)
    keep, send = pl.pallas_call(
        add_z_first_kernel,
        in_specs=whole(3),
        out_specs=whole(2),
        out_shape=[jax.ShapeDtypeStruct((4,) + part, f32), jax.ShapeDtypeStruct((5,) + part, bf16)],
        compiler_params=params(),
        name="delta_add_z_first",
    )(keep, got, mom_block)
    got = swap(send, "zh", 1)
    keep, send = pl.pallas_call(
        add_z_kernel,
        in_specs=whole(3),
        out_specs=whole(2),
        out_shape=[jax.ShapeDtypeStruct((4,) + part, f32), jax.ShapeDtypeStruct((6,) + part, bf16)],
        compiler_params=params(),
        name="delta_add_z",
    )(keep, send, got)
    return at, outgoing, keep, send


def outer_mean(keep, send, got):
    part = keep.shape[1:]
    return pl.pallas_call(
        lambda *refs: mean_kernel(32, *refs),
        in_specs=whole(3),
        out_specs=whole(1)[0],
        out_shape=jax.ShapeDtypeStruct((1, 8) + part, bf16),
        compiler_params=params(),
        name="delta_mean",
    )(keep, send, got)


def outer_finish(moe_out, at, block, global_params, momentum, local_params):
    rows, width = global_params.shape
    block = jnp.concatenate([block, swap(block, "y", 3)], axis=0)
    block = jnp.concatenate([block, swap(block, "y", 1)], axis=0)
    far = swap(block, "c", 1)
    squares = pl.pallas_call(
        square_kernel,
        in_specs=whole(2),
        out_specs=whole(1)[0],
        out_shape=jax.ShapeDtypeStruct((8, 128), f32),
        compiler_params=params(),
        name="delta_squares",
    )(block, far)
    squares = squares + swap(squares, "zl", 1)
    squares = squares + swap(squares, "x", 1)
    entries = float(rows * 8 * width)
    apart = swap(squares, "x", 3)
    apart, moe_out = lax.optimization_barrier((apart, moe_out))
    local_next, momentum_next = pl.pallas_call(
        lambda *refs: outer_kernel(entries, *refs),
        in_specs=[smem()] + whole(7),
        out_specs=whole(2),
        out_shape=[
            jax.ShapeDtypeStruct((1, rows, width), bf16),
            jax.ShapeDtypeStruct((momentum.shape[1], rows), f32),
        ],
        scratch_shapes=[pltpu.VMEM((128, 128), f32)],
        compiler_params=params(),
        name="outer_update",
    )(at, squares, apart, block, far, global_params, local_params, momentum.T)
    return momentum_next.T, local_next, moe_out


def local(
    tokens, routes, route_weight, w_gate, w_up, w_down, pseudo_grad, global_params, momentum, local_params
):
    tok_rows, feat_width = tokens.shape
    capacity = tok_rows * 3 // 8
    routes_t, weight_t = routes.T, route_weight.T
    outgoing = pl.pallas_call(
        dispatch_kernel,
        in_specs=[pl.BlockSpec(memory_space=pl.ANY)] * 2,
        out_specs=pl.BlockSpec(memory_space=pl.ANY),
        out_shape=jax.ShapeDtypeStruct((EXPERTS, capacity, feat_width), bf16),
        scratch_shapes=[
            pltpu.VMEM(routes_t.shape, jnp.int32),
            pltpu.VMEM(tokens.shape, bf16),
            pltpu.VMEM((EXPERTS, capacity, feat_width), bf16),
            pltpu.SemaphoreType.DMA((1 + 2 * (feat_width // 512),)),
        ],
        compiler_params=pltpu.CompilerParams(vmem_limit_bytes=DISPATCH_LIMIT),
        name="dispatch",
    )(routes_t, tokens)
    at, outgoing, keep, send = outer_sum(pseudo_grad, momentum, outgoing)
    received = lax.all_to_all(outgoing, SHARD, split_axis=0, concat_axis=0, tiled=True)
    received, keep, send = lax.optimization_barrier((received, keep, send))
    result = ffn(received.reshape(EXPERTS * capacity, feat_width), w_gate, w_up, w_down)
    result, got = lax.optimization_barrier((result, swap(send, "zh", 3)))
    result = result.reshape(EXPERTS, capacity, feat_width)
    returned = lax.all_to_all(result, SHARD, split_axis=0, concat_axis=0, tiled=True)
    moe_out = pl.pallas_call(
        combine_kernel,
        in_specs=whole(3),
        out_specs=whole(1)[0],
        out_shape=jax.ShapeDtypeStruct((tok_rows, feat_width), bf16),
        compiler_params=params(),
        name="combine",
    )(routes_t, weight_t, returned.reshape(EXPERTS * capacity, feat_width))
    block = outer_mean(keep, send, got)
    momentum_next, local_next, moe_out = outer_finish(moe_out, at, block, global_params, momentum, local_params)
    return (moe_out, momentum_next, local_next)


def solution(mesh):
    fine = Mesh(mesh.devices.reshape(4, 4, 2, 4, 2), REP + SHARD)
    in_specs = (
        P(REP + SHARD, None),
        P(REP + SHARD, None),
        P(REP + SHARD, None),
        P(SHARD, None, None),
        P(SHARD, None, None),
        P(SHARD, None, None),
        P(REP, SHARD, None),
        P(SHARD, None),
        P(SHARD, REP),
        P(REP, SHARD, None),
    )
    out_specs = (P(REP + SHARD, None), P(SHARD, REP), P(REP, SHARD, None))
    return jax.shard_map(local, mesh=fine, in_specs=in_specs, out_specs=out_specs, check_vma=False)
```

```python
import jax
import jax.numpy as jnp
from jax import lax
from jax.experimental import pallas as pl
from jax.experimental.pallas import tpu as pltpu
from jax.sharding import Mesh
from jax.sharding import PartitionSpec as P

f32 = jnp.float32
bf16 = jnp.bfloat16

outer_momentum = 0.9
outer_rate = 0.7
merge_weight = 0.5
clip_epsilon = 1e-06

EXPERTS = 8
REP = ("zh", "y", "c")
SHARD = ("x", "zl")
VMEM_LIMIT = 8 * 1024 * 1024
FFN_LIMIT = 52 * 1000000


def params(**more):
    return pltpu.CompilerParams(vmem_limit_bytes=VMEM_LIMIT, **more)


def whole(count):
    return [pl.BlockSpec(memory_space=pltpu.VMEM)] * count


def slots(routes, ids, capacity):
    tokens = routes.shape[1]
    named = jnp.logical_or(routes[0:1, :] == ids, routes[1:2, :] == ids)
    before = lax.broadcasted_iota(jnp.int32, (tokens, tokens), 0) < lax.broadcasted_iota(
        jnp.int32, (tokens, tokens), 1
    )
    place = jnp.dot(
        named.astype(f32).astype(bf16), before.astype(f32).astype(bf16), preferred_element_type=f32
    )
    return jnp.where(named, place.astype(jnp.int32), capacity)


def column_experts(at_ref, tokens):
    step = lax.broadcasted_iota(jnp.int32, (8, tokens), 0)
    column = jnp.bitwise_and(at_ref[4] + step, 3)
    return jnp.where(step < 4, column * 2 + at_ref[0], -1)


def one_hot(place, capacity):
    row = lax.broadcasted_iota(jnp.int32, (capacity, place.shape[1]), 0)
    return [(row == place[k : k + 1, :]).astype(f32) for k in range(4)]


def dispatch_kernel(at_ref, own_routes, far_routes, own_ref, far_ref, *out_refs):
    tokens, width = own_ref.shape[0], 512
    capacity = out_refs[0].shape[1]
    ids = column_experts(at_ref, tokens)
    for side, (routes_ref, tokens_ref) in enumerate(((own_routes, own_ref), (far_routes, far_ref))):
        place = slots(routes_ref[0:2].astype(jnp.int32), ids, capacity)
        table = jnp.concatenate(one_hot(place, capacity), axis=0).astype(bf16)
        for j in range(tokens_ref.shape[1] // width):
            cols = pl.ds(j * width, width)
            part = jnp.dot(table, tokens_ref[:, cols], preferred_element_type=f32).astype(bf16)
            for k in range(4):
                out_refs[k][side, :, cols] = part[k * capacity : (k + 1) * capacity]


def combine_kernel(at_ref, own_routes, far_routes, r0, r1, r2, r3, own_ref, far_ref, rows_ref, sems):
    refs = (r0, r1, r2, r3)
    capacity = r0.shape[1]
    tokens, width = own_ref.shape[0], 512
    copies = []
    for side in (1, 0):
        for k, ref in enumerate(refs):
            copies.append(
                pltpu.make_async_copy(
                    ref.at[side], rows_ref.at[side, pl.ds(k * capacity, capacity)], sems.at[len(copies)]
                )
            )
            copies[-1].start()
    ids = column_experts(at_ref, tokens)
    for n, (side, routes_ref, out_ref) in enumerate(((1, far_routes, far_ref), (0, own_routes, own_ref))):
        routes = routes_ref[0:2].astype(jnp.int32)
        hot = one_hot(slots(routes, ids, capacity), capacity)
        parts = []
        for k in range(4):
            weight = jnp.where(
                routes[0:1, :] == ids[k : k + 1, :], routes_ref[2:3, :], routes_ref[3:4, :]
            )
            parts.append(hot[k] * weight)
        table = jnp.concatenate(parts + [jnp.zeros((256 - 4 * capacity, tokens), f32)], axis=0).T
        table = table[:, : 4 * capacity]
        high = table.astype(bf16)
        low = (table - high.astype(f32)).astype(bf16)
        for copy in copies[4 * n : 4 * n + 4]:
            copy.wait()
        for j in range(out_ref.shape[1] // width):
            cols = pl.ds(j * width, width)
            rows = rows_ref[side, :, cols]
            out_ref[:, cols] = (
                jnp.dot(high, rows, preferred_element_type=f32)
                + jnp.dot(low, rows, preferred_element_type=f32)
            ).astype(out_ref.dtype)


def join_kernel(own_ref, got_ref, out_ref):
    out_ref[...] = (own_ref[...] + got_ref[...].astype(f32)).astype(bf16)


def ffn_kernel(*refs):
    x_hbm, (gate_hbm, up_hbm, down_hbm), out_hbm = refs[0:4], refs[4:7], refs[7:11]
    x_ref, gate_ref, up_ref, down_ref, gated_ref, hidden_ref, out_ref, sems = refs[11:]
    block, wide = 256, 512
    width, hidden = gate_ref.shape
    half, count = width // 2, hidden // block
    part_rows = x_hbm[0].shape[0]
    copies = []

    def copy(source, target):
        copies.append(pltpu.make_async_copy(source, target, sems.at[len(copies)]))
        copies[-1].start()

    for k in range(4):
        copy(x_hbm[k], x_ref.at[pl.ds(k * part_rows, part_rows)])
    for hbm, ref in ((gate_hbm, gate_ref), (up_hbm, up_ref)):
        for i in range(2):
            rows = pl.ds(i * half, half)
            copy(hbm.at[0, rows], ref.at[rows])
    copy(down_hbm.at[0], down_ref)
    for k in range(4):
        copies[k].wait()
    for i in range(2):
        rows = pl.ds(i * half, half)
        copies[4 + i].wait()
        for n in range(count):
            cols = pl.ds(n * block, block)
            part = jnp.dot(x_ref[:, rows], gate_ref[rows, cols], preferred_element_type=f32)
            gated_ref[:, cols] = part if i == 0 else gated_ref[:, cols] + part
    copies[6].wait()
    copies[7].wait()
    for n in range(count):
        cols = pl.ds(n * block, block)
        up = jnp.dot(x_ref[...], up_ref[:, cols], preferred_element_type=f32)
        gate = gated_ref[:, cols]
        hidden_ref[:, cols] = (gate / (1.0 + jnp.exp(-gate)) * up).astype(bf16)
    copies[8].wait()
    for n in range(width // wide):
        cols = pl.ds(n * wide, wide)
        out_ref[:, cols] = jnp.dot(
            hidden_ref[...], down_ref[:, cols], preferred_element_type=f32
        ).astype(bf16)
        for k in range(4):
            copy(out_ref.at[pl.ds(k * part_rows, part_rows), cols], out_hbm[k].at[:, cols])
    for out in copies[9:]:
        out.wait()


def ffn(parts, w_gate, w_up, w_down):
    part_rows, width = parts[0].shape
    rows = 4 * part_rows
    hidden = w_gate.shape[2]
    anywhere = pl.BlockSpec(memory_space=pl.ANY)
    return pl.pallas_call(
        ffn_kernel,
        in_specs=[anywhere] * 7,
        out_specs=[anywhere] * 4,
        out_shape=[jax.ShapeDtypeStruct((part_rows, width), bf16)] * 4,
        scratch_shapes=[
            pltpu.VMEM((rows, width), bf16),
            pltpu.VMEM((width, hidden), bf16),
            pltpu.VMEM((width, hidden), bf16),
            pltpu.VMEM((hidden, width), bf16),
            pltpu.VMEM((rows, hidden), f32),
            pltpu.VMEM((rows, hidden), bf16),
            pltpu.VMEM((rows, width), bf16),
            pltpu.SemaphoreType.DMA((9 + 4 * (width // 512),)),
        ],
        compiler_params=pltpu.CompilerParams(vmem_limit_bytes=FFN_LIMIT),
        cost_estimate=pl.CostEstimate(
            flops=6 * rows * width * hidden,
            bytes_accessed=6 * width * hidden + 4 * rows * width,
            transcendentals=rows * hidden,
        ),
        name="expert_ffn",
    )(*parts, w_gate, w_up, w_down)


def pieces_kernel(at_ref, own_ref, got_ref, send_ref):
    half = got_ref.shape[1]
    rows, width = send_ref.shape[1:]
    for p in range(send_ref.shape[0]):
        at_rows, first = pl.ds((p & 1) * rows, rows), (p >> 1) * width
        mine = own_ref[0, at_rows, pl.ds(pl.multiple_of(at_ref[0] * half + first, width), width)]
        send_ref[p] = (mine + got_ref[at_rows, first : first + width]).astype(bf16)


def mean_kernel(replicas, got_ref, mom_ref, out_ref):
    total = got_ref[0].astype(f32)
    for p in range(1, got_ref.shape[0]):
        total += got_ref[p].astype(f32)
    mean = (total * (1.0 / replicas)).astype(bf16)
    mom = mom_ref[...].astype(bf16)
    for p in range(out_ref.shape[0]):
        out_ref[p, 0] = mean
        out_ref[p, 1] = mom


def square_kernel(a_ref, b_ref, out_ref):
    total = jnp.zeros(out_ref.shape, f32)
    step = out_ref.shape[0]
    for ref in (a_ref, b_ref):
        for p in range(ref.shape[0]):
            block = ref[p, 0].astype(f32)
            block = block * block
            for i in range(block.shape[0] // step):
                total += block[i * step : i * step + step]
    out_ref[...] = total


def outer_kernel(entries, at_ref, near_s, far_s, near_ref, far_ref, params_ref, local_ref, mom_ref, next_ref, mom_out, scratch):
    core, rep = at_ref[0], at_ref[5]
    squares = near_s[...] + far_s[...]
    squares = jnp.sum(jnp.sum(squares, axis=1, keepdims=True), axis=0, keepdims=True)
    clip = jnp.minimum(1.0, lax.rsqrt(squares * (1.0 / entries) + clip_epsilon))

    def delta(side, piece):
        return jnp.where(core == side, near_ref[piece, 0].astype(f32), far_ref[piece, 0].astype(f32))

    for cb in range(16):
        near, far = near_ref[cb, 1].astype(f32), far_ref[cb, 1].astype(f32)
        m0, m1 = jnp.where(core == 0, near, far), jnp.where(core == 0, far, near)
        for h in range(2):
            rows, cols = pl.ds(h * 48, 48), pl.ds(cb * 128, 128)
            mom = jnp.concatenate([m0[:, h * 64 : h * 64 + 64], m1[:, h * 64 : h * 64 + 64]], axis=1)
            clipped = clip * delta(cb >> 3, (cb & 7) * 2 + h)
            after = outer_momentum * mom + clipped
            outer = params_ref[rows, cols] - outer_rate * (outer_momentum * after + clipped)
            local = local_ref[0, rows, cols].astype(f32)
            next_ref[0, rows, cols] = (merge_weight * local + (1.0 - merge_weight) * outer).astype(bf16)
    cb = jnp.right_shift(rep, 1)
    side, piece = jnp.right_shift(cb, 3), jnp.bitwise_and(cb, 7) * 2
    scratch[...] = jnp.zeros_like(scratch)
    for h in range(2):
        scratch[h * 48 : h * 48 + 48, :] = delta(side, piece + h)
    scratch[...] = scratch[...].T
    start = pl.multiple_of(core * 64, 64)
    mom_out[...] = outer_momentum * mom_ref[...] + clip * scratch[pl.ds(start, 64), 0:96]


def smem():
    return pl.BlockSpec(memory_space=pltpu.SMEM)


def swap(value, axis, bits):
    size = lax.axis_size(axis)
    return lax.ppermute(value, axis, [(i, i ^ bits) for i in range(size)])


def expert_route(step, back):
    pairs = []
    for zh in range(4):
        for y in range(4):
            for c in range(2):
                for x in range(4):
                    for zl in range(2):
                        z = 2 * zh + zl
                        to = z
                        if zl != c:
                            to = z ^ 1 if step < 2 else (z + (1 if zl else -1)) % 8
                        here = (((zh * 4 + y) * 2 + c) * 4 + x) * 2 + zl
                        there = ((((to >> 1) * 4 + y) * 2 + zl) * 4 + (x + step) % 4) * 2 + (to & 1)
                        pairs.append((there, here) if back else (here, there))
    return pairs


def expert_send(value, step, back=False):
    return lax.ppermute(value, REP + SHARD, expert_route(step, back))


def local(
    tokens, routes, route_weight, w_gate, w_up, w_down, pseudo_grad, global_params, momentum, local_params
):
    tok_rows, feat_width = tokens.shape
    capacity = tok_rows * 3 // 8
    core, y, zh = lax.axis_index("c"), lax.axis_index("y"), lax.axis_index("zh")
    x, zl = lax.axis_index("x"), lax.axis_index("zl")
    rep = (zh * 4 + y) * 2 + core
    at = jnp.stack([core, y, zh, zl, x, rep]).astype(jnp.int32)
    rows, width = pseudo_grad.shape[1:]
    half = width // 2
    part = (rows // 2, 128)

    table = jnp.concatenate([routes.T.astype(f32), route_weight.T], axis=0)
    far_tokens, far_table = swap(tokens, "c", 1), swap(table, "c", 1)
    got = swap(lax.dynamic_slice_in_dim(pseudo_grad[0], (1 - core) * half, half, 1), "c", 1)
    outgoing = pl.pallas_call(
        dispatch_kernel,
        in_specs=[smem()] + whole(4),
        out_specs=whole(4),
        out_shape=[jax.ShapeDtypeStruct((2, capacity, feat_width), bf16)] * 4,
        compiler_params=params(),
        name="dispatch",
    )(at, table, far_table, tokens, far_tokens)
    pieces = pl.pallas_call(
        pieces_kernel,
        in_specs=[smem()] + whole(2),
        out_specs=whole(1)[0],
        out_shape=jax.ShapeDtypeStruct((16,) + part, bf16),
        compiler_params=params(),
        name="delta_pieces",
    )(at, pseudo_grad, got)
    summands = lax.all_to_all(pieces, ("zh", "y"), split_axis=0, concat_axis=0, tiled=True)
    mom_block = jnp.concatenate([momentum[: rows // 2], momentum[rows // 2 :]], axis=1)
    block = pl.pallas_call(
        lambda *refs: mean_kernel(32, *refs),
        in_specs=whole(2),
        out_specs=whole(1)[0],
        out_shape=jax.ShapeDtypeStruct((16, 2) + part, bf16),
        compiler_params=params(),
        name="delta_mean",
    )(summands, mom_block)
    received = [expert_send(outgoing[k], k).reshape(2 * capacity, feat_width) for k in range(4)]
    received, block = lax.optimization_barrier((received, block))
    near = lax.all_to_all(block, ("zh", "y"), split_axis=0, concat_axis=0, tiled=True)
    result = ffn(received, w_gate, w_up, w_down)
    returned = [
        expert_send(result[k].reshape(2, capacity, feat_width), k, back=True) for k in range(4)
    ]
    far = swap(near, "c", 1)
    squares = pl.pallas_call(
        square_kernel,
        in_specs=whole(2),
        out_specs=whole(1)[0],
        out_shape=jax.ShapeDtypeStruct((8, 128), f32),
        compiler_params=params(),
        name="delta_squares",
    )(near, far)
    squares = squares + swap(squares, "zl", 1)
    squares = squares + swap(squares, "x", 1)
    returned, squares = lax.optimization_barrier((returned, squares))
    own_sum, far_sum = pl.pallas_call(
        combine_kernel,
        in_specs=[smem()] + whole(2) + [pl.BlockSpec(memory_space=pl.ANY)] * 4,
        out_specs=whole(2),
        out_shape=[jax.ShapeDtypeStruct((tok_rows, feat_width), t) for t in (f32, bf16)],
        scratch_shapes=[
            pltpu.VMEM((2, 4 * capacity, feat_width), bf16),
            pltpu.SemaphoreType.DMA((8,)),
        ],
        compiler_params=params(),
        name="combine",
    )(at, table, far_table, *returned)
    moe_out = pl.pallas_call(
        join_kernel,
        in_specs=whole(2),
        out_specs=whole(1)[0],
        out_shape=jax.ShapeDtypeStruct((tok_rows, feat_width), bf16),
        compiler_params=params(),
        name="combine_join",
    )(own_sum, swap(far_sum, "c", 1))
    entries = float(rows * 8 * width)
    local_next, momentum_next = pl.pallas_call(
        lambda *refs: outer_kernel(entries, *refs),
        in_specs=[smem()] + whole(7),
        out_specs=whole(2),
        out_shape=[
            jax.ShapeDtypeStruct((1, rows, width), bf16),
            jax.ShapeDtypeStruct((momentum.shape[1], rows), f32),
        ],
        scratch_shapes=[pltpu.VMEM((128, 128), f32)],
        compiler_params=params(),
        name="outer_update",
    )(at, squares, swap(squares, "x", 3), near, far, global_params, local_params, momentum.T)
    return (moe_out, momentum_next.T, local_next)


def solution(mesh):
    fine = Mesh(mesh.devices.reshape(4, 4, 2, 4, 2), REP + SHARD)
    in_specs = (
        P(REP + SHARD, None),
        P(REP + SHARD, None),
        P(REP + SHARD, None),
        P(SHARD, None, None),
        P(SHARD, None, None),
        P(SHARD, None, None),
        P(REP, SHARD, None),
        P(SHARD, None),
        P(SHARD, REP),
        P(REP, SHARD, None),
    )
    out_specs = (P(REP + SHARD, None), P(SHARD, REP), P(REP, SHARD, None))
    return jax.shard_map(local, mesh=fine, in_specs=in_specs, out_specs=out_specs, check_vma=False)
```

```python
import jax
import jax.numpy as jnp
from jax import lax
from jax.experimental import pallas as pl
from jax.experimental.pallas import tpu as pltpu
from jax.sharding import Mesh
from jax.sharding import PartitionSpec as P

f32 = jnp.float32
bf16 = jnp.bfloat16

outer_momentum = 0.9
outer_rate = 0.7
merge_weight = 0.5
clip_epsilon = 1e-06

EXPERTS = 8
REP = ("zh", "y", "c")
SHARD = ("x", "zl")
VMEM_LIMIT = 8 * 1024 * 1024
FFN_LIMIT = 52 * 1000000
DISPATCH_LIMIT = 58 * 1024 * 1024


def params(**more):
    return pltpu.CompilerParams(vmem_limit_bytes=VMEM_LIMIT, **more)


def whole(count):
    return [pl.BlockSpec(memory_space=pltpu.VMEM)] * count


def slots(routes, tokens, capacity):
    ids = lax.broadcasted_iota(jnp.int32, (EXPERTS, tokens), 0)
    named = jnp.logical_or(routes[0:1, :] == ids, routes[1:2, :] == ids)
    before = lax.broadcasted_iota(jnp.int32, (tokens, tokens), 0) < lax.broadcasted_iota(
        jnp.int32, (tokens, tokens), 1
    )
    place = jnp.dot(
        named.astype(f32).astype(bf16), before.astype(f32).astype(bf16), preferred_element_type=f32
    )
    return jnp.where(named, place.astype(jnp.int32), capacity)


def dispatch_kernel(
    routes_hbm, tokens_hbm, weight_hbm, out_hbm, routes_ref, weight_ref, tokens_ref, out_ref, sems
):
    tokens = tokens_ref.shape[0]
    capacity = out_ref.shape[1]
    width = 512
    parts = [pl.ds(j * width, width) for j in range(tokens_ref.shape[1] // width)]
    first = pltpu.make_async_copy(routes_hbm, routes_ref, sems.at[0])
    first.start()
    last = pltpu.make_async_copy(weight_hbm, weight_ref, sems.at[1 + 2 * len(parts)])
    last.start()
    reads = [
        pltpu.make_async_copy(tokens_hbm.at[:, cols], tokens_ref.at[:, cols], sems.at[1 + j])
        for j, cols in enumerate(parts)
    ]
    for copy in reads:
        copy.start()
    first.wait()
    place = slots(routes_ref[...], tokens, capacity)
    row = lax.broadcasted_iota(jnp.int32, (capacity, tokens), 0)
    table = jnp.concatenate(
        [(row == place[e : e + 1, :]).astype(f32) for e in range(EXPERTS)], axis=0
    ).astype(bf16)
    writes = []
    for j, cols in enumerate(parts):
        reads[j].wait()
        part = jnp.dot(table, tokens_ref[:, cols], preferred_element_type=f32).astype(bf16)
        out_ref[:, :, cols] = part.reshape(EXPERTS, capacity, width)
        writes.append(
            pltpu.make_async_copy(out_ref.at[:, :, cols], out_hbm.at[:, :, cols], sems.at[1 + len(parts) + j])
        )
        writes[-1].start()
    for copy in writes + [last]:
        copy.wait()


def combine_kernel(routes_ref, weight_ref, rows_ref, out_ref):
    tokens = routes_ref.shape[1]
    capacity = rows_ref.shape[0] // EXPERTS
    routes = routes_ref[...]
    place = slots(routes, tokens, capacity)
    row = lax.broadcasted_iota(jnp.int32, (capacity, tokens), 0)
    parts = []
    for e in range(EXPERTS):
        weight = jnp.where(routes[0:1, :] == e, weight_ref[0:1, :], weight_ref[1:2, :])
        parts.append(jnp.where(row == place[e : e + 1, :], weight, 0.0))
    table = jnp.concatenate(parts, axis=0).T
    high = table.astype(bf16)
    low = (table - high.astype(f32)).astype(bf16)
    width = 512
    for j in range(out_ref.shape[1] // width):
        cols = pl.ds(j * width, width)
        rows = rows_ref[:, cols]
        out_ref[:, cols] = (
            jnp.dot(high, rows, preferred_element_type=f32)
            + jnp.dot(low, rows, preferred_element_type=f32)
        ).astype(bf16)


def ffn_kernel(
    x_ref, gate_hbm, up_hbm, down_hbm, out_hbm, gate_ref, up_ref, down_ref, gated_ref, hidden_ref, out_ref, sems
):
    block, wide = 256, 512
    width, hidden = gate_ref.shape
    half, count = width // 2, hidden // block
    copies = []
    for hbm, ref in ((gate_hbm, gate_ref), (up_hbm, up_ref)):
        for i in range(2):
            rows = pl.ds(i * half, half)
            copies.append(pltpu.make_async_copy(hbm.at[0, rows], ref.at[rows], sems.at[len(copies)]))
    copies.append(pltpu.make_async_copy(down_hbm.at[0], down_ref, sems.at[4]))
    for copy in copies:
        copy.start()
    for i in range(2):
        rows = pl.ds(i * half, half)
        copies[i].wait()
        for n in range(count):
            cols = pl.ds(n * block, block)
            part = jnp.dot(x_ref[:, rows], gate_ref[rows, cols], preferred_element_type=f32)
            gated_ref[:, cols] = part if i == 0 else gated_ref[:, cols] + part
    copies[2].wait()
    copies[3].wait()
    for n in range(count):
        cols = pl.ds(n * block, block)
        up = jnp.dot(x_ref[...], up_ref[:, cols], preferred_element_type=f32)
        gate = gated_ref[:, cols]
        hidden_ref[:, cols] = (gate / (1.0 + jnp.exp(-gate)) * up).astype(bf16)
    copies[4].wait()
    results = []
    for n in range(width // wide):
        cols = pl.ds(n * wide, wide)
        out_ref[:, cols] = jnp.dot(
            hidden_ref[...], down_ref[:, cols], preferred_element_type=f32
        ).astype(bf16)
        results.append(pltpu.make_async_copy(out_ref.at[:, cols], out_hbm.at[:, cols], sems.at[5 + n]))
        results[-1].start()
    for copy in results:
        copy.wait()


def ffn(x, w_gate, w_up, w_down):
    rows, width = x.shape
    hidden = w_gate.shape[2]
    anywhere = pl.BlockSpec(memory_space=pl.ANY)
    return pl.pallas_call(
        ffn_kernel,
        in_specs=whole(1) + [anywhere] * 3,
        out_specs=anywhere,
        out_shape=jax.ShapeDtypeStruct((rows, width), bf16),
        scratch_shapes=[
            pltpu.VMEM((width, hidden), bf16),
            pltpu.VMEM((width, hidden), bf16),
            pltpu.VMEM((hidden, width), bf16),
            pltpu.VMEM((rows, hidden), f32),
            pltpu.VMEM((rows, hidden), bf16),
            pltpu.VMEM((rows, width), bf16),
            pltpu.SemaphoreType.DMA((5 + width // 512,)),
        ],
        compiler_params=pltpu.CompilerParams(vmem_limit_bytes=FFN_LIMIT),
        cost_estimate=pl.CostEstimate(
            flops=6 * rows * width * hidden,
            bytes_accessed=6 * width * hidden + 4 * rows * width,
            transcendentals=rows * hidden,
        ),
        name="expert_ffn",
    )(x, w_gate, w_up, w_down)


def halve_first_kernel(at_ref, own_ref, got_ref, mom_ref, keep_ref, send_ref, scratch):
    core, bit = at_ref[0], at_ref[1]
    half, (count, rows, width) = got_ref.shape[1], keep_ref.shape
    for ref, which in ((send_ref, 1 - bit), (keep_ref, bit)):
        for b in range(count):
            at_rows, first = pl.ds((b & 1) * rows, rows), which * (half // 2) + (b >> 1) * width
            mine = own_ref[0, at_rows, pl.ds(pl.multiple_of(core * half + first, width), width)]
            other = got_ref[at_rows, pl.ds(pl.multiple_of(first, width), width)]
            ref[b] = (mine + other).astype(ref.dtype)
    wide, tall = mom_ref.shape
    scratch[...] = jnp.zeros_like(scratch)
    scratch[0:wide, 0:tall] = mom_ref[...]
    mom = scratch[...].T
    mom = jnp.concatenate([mom[0:rows, 0:wide], mom[rows : 2 * rows, 0:wide]], axis=1)
    send_ref[count] = mom.astype(bf16)


def halve_kernel(at_ref, own_ref, sent_ref, got_ref, keep_ref, send_ref):
    bit, count = at_ref[2], keep_ref.shape[0]
    for ref, which in ((send_ref, 1 - bit), (keep_ref, bit)):
        for b in range(count):
            i = which * count + b
            ref[b] = (own_ref[i] + got_ref[i].astype(f32)).astype(ref.dtype)
    send_ref[count] = sent_ref[2 * count]
    send_ref[count + 1] = got_ref[2 * count]


def add_z_kernel(own_ref, sent_ref, got_ref, keep_ref, send_ref):
    count, held = keep_ref.shape[0], sent_ref.shape[0] - keep_ref.shape[0]
    total = own_ref[...] + got_ref[0:count].astype(f32)
    keep_ref[...] = total
    send_ref[0:count] = total.astype(bf16)
    send_ref[count : count + held] = sent_ref[count:]
    send_ref[count + held :] = got_ref[count:]


def mean_kernel(replicas, own_ref, sent_ref, got_ref, out_ref, mom_ref):
    count, held = own_ref.shape[0], sent_ref.shape[0] - own_ref.shape[0]
    total = own_ref[...] + got_ref[0:count].astype(f32)
    out_ref[0] = (total * (1.0 / replicas)).astype(bf16)
    mom_ref[0:held] = sent_ref[count:]
    mom_ref[held:] = got_ref[count:]


def square_kernel(a_ref, b_ref, out_ref):
    total = jnp.zeros(out_ref.shape, f32)
    step = out_ref.shape[0]
    for ref in (a_ref, b_ref):
        for j in range(4):
            for k in range(4):
                block = ref[j, k].astype(f32)
                block = block * block
                for i in range(block.shape[0] // step):
                    total += block[i * step : i * step + step]
    out_ref[...] = total


def quarter_of(y):
    return ((y & 1) ^ (y >> 1)) * 2 + (y >> 1)


def flips(apart):
    high = jnp.right_shift(apart, 1)
    return high * 2 + jnp.bitwise_xor(jnp.bitwise_and(apart, 1), high)


def outer_kernel(
    entries, at_ref, near_s, far_s, near_ref, far_ref, near_m, far_m, params_ref, local_ref, mom_ref, next_ref, mom_out, scratch
):
    core, quarter, zh, rep, y = at_ref[0], at_ref[3], at_ref[4], at_ref[5], at_ref[6]
    squares = near_s[...] + far_s[...]
    squares = jnp.sum(jnp.sum(squares, axis=1, keepdims=True), axis=0, keepdims=True)
    clip = jnp.minimum(1.0, lax.rsqrt(squares * (1.0 / entries) + clip_epsilon))

    def delta(side, piece, slot):
        j = jnp.bitwise_xor(piece, quarter)
        return jnp.where(
            core == side, near_ref[j, slot].astype(f32), far_ref[j, slot].astype(f32)
        )

    for cb in range(16):
        slot = flips(jnp.bitwise_xor(zh, cb >> 2)) * 4 + flips(jnp.bitwise_xor(y, cb & 3))
        near, far = near_m[slot].astype(f32), far_m[slot].astype(f32)
        m0, m1 = jnp.where(core == 0, near, far), jnp.where(core == 0, far, near)
        for h in range(2):
            rows, cols = pl.ds(h * 48, 48), pl.ds(cb * 128, 128)
            mom = jnp.concatenate([m0[:, h * 64 : h * 64 + 64], m1[:, h * 64 : h * 64 + 64]], axis=1)
            clipped = clip * delta(cb >> 3, (cb >> 1) & 3, (cb & 1) * 2 + h)
            after = outer_momentum * mom + clipped
            outer = params_ref[rows, cols] - outer_rate * (outer_momentum * after + clipped)
            local = local_ref[0, rows, cols].astype(f32)
            next_ref[0, rows, cols] = (merge_weight * local + (1.0 - merge_weight) * outer).astype(bf16)
    cb = jnp.right_shift(rep, 1)
    side, piece = jnp.right_shift(cb, 3), jnp.bitwise_and(jnp.right_shift(cb, 1), 3)
    scratch[...] = jnp.zeros_like(scratch)
    for h in range(2):
        scratch[h * 48 : h * 48 + 48, :] = delta(side, piece, jnp.bitwise_and(cb, 1) * 2 + h)
    scratch[...] = scratch[...].T
    start = pl.multiple_of(core * 64, 64)
    mom_out[...] = outer_momentum * mom_ref[...] + clip * scratch[pl.ds(start, 64), 0:96]


def smem():
    return pl.BlockSpec(memory_space=pltpu.SMEM)


def swap(value, axis, bits):
    size = lax.axis_size(axis)
    return lax.ppermute(value, axis, [(i, i ^ bits) for i in range(size)])


def outer_sum(pseudo_grad, momentum, outgoing):
    rows, width = pseudo_grad.shape[1:]
    core, y, zh = lax.axis_index("c"), lax.axis_index("y"), lax.axis_index("zh")
    rep = (zh * 4 + y) * 2 + core
    first, second = (y & 1) ^ (y >> 1), y >> 1
    at = jnp.stack([core, first, second, first * 2 + second, zh, rep, y]).astype(jnp.int32)
    half = width // 2
    part = (rows // 2, 128)

    def pair(held, sent):
        return [jax.ShapeDtypeStruct((held,) + part, f32), jax.ShapeDtypeStruct((sent,) + part, bf16)]

    got = swap(lax.dynamic_slice_in_dim(pseudo_grad[0], (1 - core) * half, half, 1), "c", 1)
    keep, send = pl.pallas_call(
        halve_first_kernel,
        in_specs=[smem()] + whole(3),
        out_specs=whole(2),
        out_shape=pair(8, 9),
        scratch_shapes=[pltpu.VMEM((128, 128), f32)],
        compiler_params=params(),
        name="delta_halve_first",
    )(at, pseudo_grad, got, momentum.T)
    outgoing, keep, send = lax.optimization_barrier((outgoing, keep, send))
    got = swap(send, "y", 1)
    keep, send = pl.pallas_call(
        halve_kernel,
        in_specs=[smem()] + whole(3),
        out_specs=whole(2),
        out_shape=pair(4, 6),
        compiler_params=params(),
        name="delta_halve",
    )(at, keep, send, got)
    for axis, bits, sent in (("y", 3, 8), ("zh", 1, 12)):
        got = swap(send, axis, bits)
        keep, send = pl.pallas_call(
            add_z_kernel,
            in_specs=whole(3),
            out_specs=whole(2),
            out_shape=pair(4, sent),
            compiler_params=params(),
            name="delta_add_" + axis,
        )(keep, send, got)
    return at, outgoing, keep, send


def outer_mean(keep, send, got):
    part = keep.shape[1:]
    return pl.pallas_call(
        lambda *refs: mean_kernel(32, *refs),
        in_specs=whole(3),
        out_specs=whole(2),
        out_shape=[
            jax.ShapeDtypeStruct((1, 4) + part, bf16),
            jax.ShapeDtypeStruct((16,) + part, bf16),
        ],
        compiler_params=params(),
        name="delta_mean",
    )(keep, send, got)


def outer_finish(moe_out, at, block, mom_near, global_params, momentum, local_params):
    rows, width = global_params.shape
    mom_far = swap(mom_near, "c", 1)
    block = jnp.concatenate([block, swap(block, "y", 3)], axis=0)
    block = jnp.concatenate([block, swap(block, "y", 1)], axis=0)
    far = swap(block, "c", 1)
    squares = pl.pallas_call(
        square_kernel,
        in_specs=whole(2),
        out_specs=whole(1)[0],
        out_shape=jax.ShapeDtypeStruct((8, 128), f32),
        compiler_params=params(),
        name="delta_squares",
    )(block, far)
    squares = squares + swap(squares, "zl", 1)
    squares = squares + swap(squares, "x", 1)
    entries = float(rows * 8 * width)
    apart = swap(squares, "x", 3)
    apart, moe_out = lax.optimization_barrier((apart, moe_out))
    local_next, momentum_next = pl.pallas_call(
        lambda *refs: outer_kernel(entries, *refs),
        in_specs=[smem()] + whole(9),
        out_specs=whole(2),
        out_shape=[
            jax.ShapeDtypeStruct((1, rows, width), bf16),
            jax.ShapeDtypeStruct((momentum.shape[1], rows), f32),
        ],
        scratch_shapes=[pltpu.VMEM((128, 128), f32)],
        compiler_params=params(),
        name="outer_update",
    )(at, squares, apart, block, far, mom_near, mom_far, global_params, local_params, momentum.T)
    return momentum_next.T, local_next, moe_out


def local(
    tokens, routes, route_weight, w_gate, w_up, w_down, pseudo_grad, global_params, momentum, local_params
):
    tok_rows, feat_width = tokens.shape
    capacity = tok_rows * 3 // 8
    routes_t, weight_t = routes.T, route_weight.T
    outgoing, routes_t, weight_t = pl.pallas_call(
        dispatch_kernel,
        in_specs=[pl.BlockSpec(memory_space=pl.ANY)] * 3,
        out_specs=[pl.BlockSpec(memory_space=pl.ANY)] + whole(2),
        out_shape=[
            jax.ShapeDtypeStruct((EXPERTS, capacity, feat_width), bf16),
            jax.ShapeDtypeStruct(routes_t.shape, jnp.int32),
            jax.ShapeDtypeStruct(weight_t.shape, f32),
        ],
        scratch_shapes=[
            pltpu.VMEM(tokens.shape, bf16),
            pltpu.VMEM((EXPERTS, capacity, feat_width), bf16),
            pltpu.SemaphoreType.DMA((2 + 2 * (feat_width // 512),)),
        ],
        compiler_params=pltpu.CompilerParams(vmem_limit_bytes=DISPATCH_LIMIT),
        name="dispatch",
    )(routes_t, tokens, weight_t)
    at, outgoing, keep, send = outer_sum(pseudo_grad, momentum, outgoing)
    received = lax.all_to_all(outgoing, SHARD, split_axis=0, concat_axis=0, tiled=True)
    received, keep, send = lax.optimization_barrier((received, keep, send))
    result = ffn(received.reshape(EXPERTS * capacity, feat_width), w_gate, w_up, w_down)
    result, got = lax.optimization_barrier((result, swap(send, "zh", 3)))
    result = result.reshape(EXPERTS, capacity, feat_width)
    returned = lax.all_to_all(result, SHARD, split_axis=0, concat_axis=0, tiled=True)
    moe_out = pl.pallas_call(
        combine_kernel,
        in_specs=whole(3),
        out_specs=whole(1)[0],
        out_shape=jax.ShapeDtypeStruct((tok_rows, feat_width), bf16),
        compiler_params=params(),
        name="combine",
    )(routes_t, weight_t, returned.reshape(EXPERTS * capacity, feat_width))
    block, mom_near = outer_mean(keep, send, got)
    momentum_next, local_next, moe_out = outer_finish(moe_out, at, block, mom_near, global_params, momentum, local_params)
    return (moe_out, momentum_next, local_next)


def solution(mesh):
    fine = Mesh(mesh.devices.reshape(4, 4, 2, 4, 2), REP + SHARD)
    in_specs = (
        P(REP + SHARD, None),
        P(REP + SHARD, None),
        P(REP + SHARD, None),
        P(SHARD, None, None),
        P(SHARD, None, None),
        P(SHARD, None, None),
        P(REP, SHARD, None),
        P(SHARD, None),
        P(SHARD, REP),
        P(REP, SHARD, None),
    )
    out_specs = (P(REP + SHARD, None), P(SHARD, REP), P(REP, SHARD, None))
    return jax.shard_map(local, mesh=fine, in_specs=in_specs, out_specs=out_specs, check_vma=False)
```

```python
import jax
import jax.numpy as jnp
from jax import lax
from jax.experimental import pallas as pl
from jax.experimental.pallas import tpu as pltpu
from jax.sharding import Mesh
from jax.sharding import PartitionSpec as P

f32 = jnp.float32
bf16 = jnp.bfloat16

outer_momentum = 0.9
outer_rate = 0.7
merge_weight = 0.5
clip_epsilon = 1e-06

EXPERTS = 8
REP = ("zh", "y", "c")
SHARD = ("x", "zl")
VMEM_LIMIT = 8 * 1024 * 1024
FFN_LIMIT = 52 * 1000000
DISPATCH_LIMIT = 58 * 1024 * 1024


def params(**more):
    return pltpu.CompilerParams(vmem_limit_bytes=VMEM_LIMIT, **more)


def whole(count):
    return [pl.BlockSpec(memory_space=pltpu.VMEM)] * count


def slots(routes, tokens, capacity):
    ids = lax.broadcasted_iota(jnp.int32, (EXPERTS, tokens), 0)
    named = jnp.logical_or(routes[0:1, :] == ids, routes[1:2, :] == ids)
    before = lax.broadcasted_iota(jnp.int32, (tokens, tokens), 0) < lax.broadcasted_iota(
        jnp.int32, (tokens, tokens), 1
    )
    place = jnp.dot(
        named.astype(f32).astype(bf16), before.astype(f32).astype(bf16), preferred_element_type=f32
    )
    return jnp.where(named, place.astype(jnp.int32), capacity)


def dispatch_kernel(routes_hbm, tokens_hbm, out_hbm, routes_ref, tokens_ref, out_ref, sems):
    tokens = tokens_ref.shape[0]
    capacity = out_ref.shape[1]
    width = 512
    parts = [pl.ds(j * width, width) for j in range(tokens_ref.shape[1] // width)]
    first = pltpu.make_async_copy(routes_hbm, routes_ref, sems.at[0])
    first.start()
    reads = [
        pltpu.make_async_copy(tokens_hbm.at[:, cols], tokens_ref.at[:, cols], sems.at[1 + j])
        for j, cols in enumerate(parts)
    ]
    for copy in reads:
        copy.start()
    first.wait()
    place = slots(routes_ref[...], tokens, capacity)
    row = lax.broadcasted_iota(jnp.int32, (capacity, tokens), 0)
    table = jnp.concatenate(
        [(row == place[e : e + 1, :]).astype(f32) for e in range(EXPERTS)], axis=0
    ).astype(bf16)
    writes = []
    for j, cols in enumerate(parts):
        reads[j].wait()
        part = jnp.dot(table, tokens_ref[:, cols], preferred_element_type=f32).astype(bf16)
        out_ref[:, :, cols] = part.reshape(EXPERTS, capacity, width)
        writes.append(
            pltpu.make_async_copy(out_ref.at[:, :, cols], out_hbm.at[:, :, cols], sems.at[1 + len(parts) + j])
        )
        writes[-1].start()
    for copy in writes:
        copy.wait()


def combine_kernel(routes_ref, weight_ref, rows_ref, out_ref):
    tokens = routes_ref.shape[1]
    capacity = rows_ref.shape[0] // EXPERTS
    routes = routes_ref[...]
    place = slots(routes, tokens, capacity)
    row = lax.broadcasted_iota(jnp.int32, (capacity, tokens), 0)
    parts = []
    for e in range(EXPERTS):
        weight = jnp.where(routes[0:1, :] == e, weight_ref[0:1, :], weight_ref[1:2, :])
        parts.append(jnp.where(row == place[e : e + 1, :], weight, 0.0))
    table = jnp.concatenate(parts, axis=0).T
    high = table.astype(bf16)
    low = (table - high.astype(f32)).astype(bf16)
    width = 512
    for j in range(out_ref.shape[1] // width):
        cols = pl.ds(j * width, width)
        rows = rows_ref[:, cols]
        out_ref[:, cols] = (
            jnp.dot(high, rows, preferred_element_type=f32)
            + jnp.dot(low, rows, preferred_element_type=f32)
        ).astype(bf16)


def ffn_kernel(
    x_ref, gate_hbm, up_hbm, down_hbm, out_hbm, gate_ref, up_ref, down_ref, gated_ref, hidden_ref, out_ref, sems
):
    block, wide = 256, 512
    width, hidden = gate_ref.shape
    half, count = width // 2, hidden // block
    copies = []
    for hbm, ref in ((gate_hbm, gate_ref), (up_hbm, up_ref)):
        for i in range(2):
            rows = pl.ds(i * half, half)
            copies.append(pltpu.make_async_copy(hbm.at[0, rows], ref.at[rows], sems.at[len(copies)]))
    copies.append(pltpu.make_async_copy(down_hbm.at[0], down_ref, sems.at[4]))
    for copy in copies:
        copy.start()
    for i in range(2):
        rows = pl.ds(i * half, half)
        copies[i].wait()
        for n in range(count):
            cols = pl.ds(n * block, block)
            part = jnp.dot(x_ref[:, rows], gate_ref[rows, cols], preferred_element_type=f32)
            gated_ref[:, cols] = part if i == 0 else gated_ref[:, cols] + part
    copies[2].wait()
    copies[3].wait()
    for n in range(count):
        cols = pl.ds(n * block, block)
        up = jnp.dot(x_ref[...], up_ref[:, cols], preferred_element_type=f32)
        gate = gated_ref[:, cols]
        hidden_ref[:, cols] = (gate / (1.0 + jnp.exp(-gate)) * up).astype(bf16)
    copies[4].wait()
    results = []
    for n in range(width // wide):
        cols = pl.ds(n * wide, wide)
        out_ref[:, cols] = jnp.dot(
            hidden_ref[...], down_ref[:, cols], preferred_element_type=f32
        ).astype(bf16)
        results.append(pltpu.make_async_copy(out_ref.at[:, cols], out_hbm.at[:, cols], sems.at[5 + n]))
        results[-1].start()
    for copy in results:
        copy.wait()


def ffn(x, w_gate, w_up, w_down):
    rows, width = x.shape
    hidden = w_gate.shape[2]
    anywhere = pl.BlockSpec(memory_space=pl.ANY)
    return pl.pallas_call(
        ffn_kernel,
        in_specs=whole(1) + [anywhere] * 3,
        out_specs=anywhere,
        out_shape=jax.ShapeDtypeStruct((rows, width), bf16),
        scratch_shapes=[
            pltpu.VMEM((width, hidden), bf16),
            pltpu.VMEM((width, hidden), bf16),
            pltpu.VMEM((hidden, width), bf16),
            pltpu.VMEM((rows, hidden), f32),
            pltpu.VMEM((rows, hidden), bf16),
            pltpu.VMEM((rows, width), bf16),
            pltpu.SemaphoreType.DMA((5 + width // 512,)),
        ],
        compiler_params=pltpu.CompilerParams(vmem_limit_bytes=FFN_LIMIT),
        cost_estimate=pl.CostEstimate(
            flops=6 * rows * width * hidden,
            bytes_accessed=6 * width * hidden + 4 * rows * width,
            transcendentals=rows * hidden,
        ),
        name="expert_ffn",
    )(x, w_gate, w_up, w_down)


def halve_first_kernel(at_ref, own_ref, got_ref, keep_ref, send_ref):
    core, bit = at_ref[0], at_ref[1]
    half, width = got_ref.shape[1], keep_ref.shape[1]
    for ref, which in ((send_ref, 1 - bit), (keep_ref, bit)):
        mine = own_ref[0, :, pl.ds(pl.multiple_of(core * half + which * width, width), width)]
        other = got_ref[:, pl.ds(pl.multiple_of(which * width, width), width)]
        ref[...] = (mine + other).astype(ref.dtype)


def halve_kernel(at_ref, own_ref, got_ref, keep_ref, send_ref):
    bit, width = at_ref[2], keep_ref.shape[1]
    for ref, which in ((send_ref, 1 - bit), (keep_ref, bit)):
        cols = pl.ds(pl.multiple_of(which * width, width), width)
        ref[...] = (own_ref[:, cols] + got_ref[:, cols].astype(f32)).astype(ref.dtype)


def add_z_first_kernel(own_ref, got_ref, mom_ref, keep_ref, send_ref):
    rows = send_ref.shape[1]
    total = own_ref[...] + got_ref[...].astype(f32)
    for p in range(4):
        keep_ref[p] = total[(p & 1) * rows : (p & 1) * rows + rows, (p >> 1) * 128 : (p >> 1) * 128 + 128]
    send_ref[0:4] = keep_ref[...].astype(bf16)
    send_ref[4] = mom_ref[...].astype(bf16)


def add_z_kernel(own_ref, sent_ref, got_ref, keep_ref, send_ref):
    total = own_ref[...] + got_ref[0:4].astype(f32)
    keep_ref[...] = total
    send_ref[0:4] = total.astype(bf16)
    send_ref[4] = sent_ref[4]
    send_ref[5] = got_ref[4]


def mean_kernel(replicas, own_ref, sent_ref, got_ref, out_ref):
    total = own_ref[...] + got_ref[0:4].astype(f32)
    out_ref[0, 0:4] = (total * (1.0 / replicas)).astype(bf16)
    out_ref[0, 4:6] = sent_ref[4:6]
    out_ref[0, 6:8] = got_ref[4:6]


def square_kernel(a_ref, b_ref, out_ref):
    total = jnp.zeros(out_ref.shape, f32)
    step = out_ref.shape[0]
    for ref in (a_ref, b_ref):
        for j in range(4):
            for k in range(4):
                block = ref[j, k].astype(f32)
                block = block * block
                for i in range(block.shape[0] // step):
                    total += block[i * step : i * step + step]
    out_ref[...] = total


def quarter_of(y):
    return ((y & 1) ^ (y >> 1)) * 2 + (y >> 1)


def outer_kernel(entries, at_ref, near_s, far_s, near_ref, far_ref, params_ref, local_ref, mom_ref, next_ref, mom_out, scratch):
    core, quarter, zh, rep = at_ref[0], at_ref[3], at_ref[4], at_ref[5]
    squares = near_s[...] + far_s[...]
    squares = jnp.sum(jnp.sum(squares, axis=1, keepdims=True), axis=0, keepdims=True)
    clip = jnp.minimum(1.0, lax.rsqrt(squares * (1.0 / entries) + clip_epsilon))

    def delta(side, piece, slot):
        j = jnp.bitwise_xor(piece, quarter)
        return jnp.where(
            core == side, near_ref[j, slot].astype(f32), far_ref[j, slot].astype(f32)
        )

    for cb in range(16):
        j = jnp.bitwise_xor(quarter_of(cb & 3), quarter)
        apart = jnp.bitwise_xor(zh, cb >> 2)
        high = jnp.right_shift(apart, 1)
        slot = 4 + high * 2 + jnp.bitwise_xor(jnp.bitwise_and(apart, 1), high)
        near, far = near_ref[j, slot].astype(f32), far_ref[j, slot].astype(f32)
        m0, m1 = jnp.where(core == 0, near, far), jnp.where(core == 0, far, near)
        for h in range(2):
            rows, cols = pl.ds(h * 48, 48), pl.ds(cb * 128, 128)
            mom = jnp.concatenate([m0[:, h * 64 : h * 64 + 64], m1[:, h * 64 : h * 64 + 64]], axis=1)
            clipped = clip * delta(cb >> 3, (cb >> 1) & 3, (cb & 1) * 2 + h)
            after = outer_momentum * mom + clipped
            outer = params_ref[rows, cols] - outer_rate * (outer_momentum * after + clipped)
            local = local_ref[0, rows, cols].astype(f32)
            next_ref[0, rows, cols] = (merge_weight * local + (1.0 - merge_weight) * outer).astype(bf16)
    cb = jnp.right_shift(rep, 1)
    side, piece = jnp.right_shift(cb, 3), jnp.bitwise_and(jnp.right_shift(cb, 1), 3)
    scratch[...] = jnp.zeros_like(scratch)
    for h in range(2):
        scratch[h * 48 : h * 48 + 48, :] = delta(side, piece, jnp.bitwise_and(cb, 1) * 2 + h)
    scratch[...] = scratch[...].T
    start = pl.multiple_of(core * 64, 64)
    mom_out[...] = outer_momentum * mom_ref[...] + clip * scratch[pl.ds(start, 64), 0:96]


def smem():
    return pl.BlockSpec(memory_space=pltpu.SMEM)


def swap(value, axis, bits):
    size = lax.axis_size(axis)
    return lax.ppermute(value, axis, [(i, i ^ bits) for i in range(size)])


def outer_sum(pseudo_grad, momentum):
    rows, width = pseudo_grad.shape[1:]
    core, y, zh = lax.axis_index("c"), lax.axis_index("y"), lax.axis_index("zh")
    rep = (zh * 4 + y) * 2 + core
    first, second = (y & 1) ^ (y >> 1), y >> 1
    at = jnp.stack([core, first, second, first * 2 + second, zh, rep]).astype(jnp.int32)
    half = width // 2
    got = swap(lax.dynamic_slice_in_dim(pseudo_grad[0], (1 - core) * half, half, 1), "c", 1)
    keep, send = pl.pallas_call(
        halve_first_kernel,
        in_specs=[smem()] + whole(2),
        out_specs=whole(2),
        out_shape=[jax.ShapeDtypeStruct((rows, half // 2), t) for t in (f32, bf16)],
        compiler_params=params(),
        name="delta_halve_first",
    )(at, pseudo_grad, got)
    got = swap(send, "y", 1)
    keep, send = pl.pallas_call(
        halve_kernel,
        in_specs=[smem()] + whole(2),
        out_specs=whole(2),
        out_shape=[jax.ShapeDtypeStruct((rows, half // 4), t) for t in (f32, bf16)],
        compiler_params=params(),
        name="delta_halve",
    )(at, keep, got)
    got = swap(send, "y", 3)
    part = (rows // 2, half // 8)
    mom_block = jnp.concatenate([momentum[: rows // 2], momentum[rows // 2 :]], axis=1)
    keep, send = pl.pallas_call(
        add_z_first_kernel,
        in_specs=whole(3),
        out_specs=whole(2),
        out_shape=[jax.ShapeDtypeStruct((4,) + part, f32), jax.ShapeDtypeStruct((5,) + part, bf16)],
        compiler_params=params(),
        name="delta_add_z_first",
    )(keep, got, mom_block)
    got = swap(send, "zh", 1)
    keep, send = pl.pallas_call(
        add_z_kernel,
        in_specs=whole(3),
        out_specs=whole(2),
        out_shape=[jax.ShapeDtypeStruct((4,) + part, f32), jax.ShapeDtypeStruct((6,) + part, bf16)],
        compiler_params=params(),
        name="delta_add_z",
    )(keep, send, got)
    return at, keep, send


def outer_mean(keep, send, got):
    part = keep.shape[1:]
    return pl.pallas_call(
        lambda *refs: mean_kernel(32, *refs),
        in_specs=whole(3),
        out_specs=whole(1)[0],
        out_shape=jax.ShapeDtypeStruct((1, 8) + part, bf16),
        compiler_params=params(),
        name="delta_mean",
    )(keep, send, got)


def outer_finish(moe_out, at, block, global_params, momentum, local_params):
    rows, width = global_params.shape
    block = jnp.concatenate([block, swap(block, "y", 3)], axis=0)
    block = jnp.concatenate([block, swap(block, "y", 1)], axis=0)
    far = swap(block, "c", 1)
    squares = pl.pallas_call(
        square_kernel,
        in_specs=whole(2),
        out_specs=whole(1)[0],
        out_shape=jax.ShapeDtypeStruct((8, 128), f32),
        compiler_params=params(),
        name="delta_squares",
    )(block, far)
    squares = squares + lax.ppermute(
        squares, ("zh", "zl"), [(z, (z + 1 if z % 2 else z - 1) % 8) for z in range(8)]
    )
    squares = squares + swap(squares, "x", 1)
    entries = float(rows * 8 * width)
    apart = swap(squares, "x", 3)
    apart, moe_out = lax.optimization_barrier((apart, moe_out))
    local_next, momentum_next = pl.pallas_call(
        lambda *refs: outer_kernel(entries, *refs),
        in_specs=[smem()] + whole(7),
        out_specs=whole(2),
        out_shape=[
            jax.ShapeDtypeStruct((1, rows, width), bf16),
            jax.ShapeDtypeStruct((momentum.shape[1], rows), f32),
        ],
        scratch_shapes=[pltpu.VMEM((128, 128), f32)],
        compiler_params=params(),
        name="outer_update",
    )(at, squares, apart, block, far, global_params, local_params, momentum.T)
    return momentum_next.T, local_next, moe_out


def local(
    tokens, routes, route_weight, w_gate, w_up, w_down, pseudo_grad, global_params, momentum, local_params
):
    tok_rows, feat_width = tokens.shape
    capacity = tok_rows * 3 // 8
    routes_t, weight_t = routes.T, route_weight.T
    outgoing = pl.pallas_call(
        dispatch_kernel,
        in_specs=[pl.BlockSpec(memory_space=pl.ANY)] * 2,
        out_specs=pl.BlockSpec(memory_space=pl.ANY),
        out_shape=jax.ShapeDtypeStruct((EXPERTS, capacity, feat_width), bf16),
        scratch_shapes=[
            pltpu.VMEM(routes_t.shape, jnp.int32),
            pltpu.VMEM(tokens.shape, bf16),
            pltpu.VMEM((EXPERTS, capacity, feat_width), bf16),
            pltpu.SemaphoreType.DMA((1 + 2 * (feat_width // 512),)),
        ],
        compiler_params=pltpu.CompilerParams(vmem_limit_bytes=DISPATCH_LIMIT),
        name="dispatch",
    )(routes_t, tokens)
    at, keep, send = outer_sum(pseudo_grad, momentum)
    received = lax.all_to_all(outgoing, SHARD, split_axis=0, concat_axis=0, tiled=True)
    received, keep, send = lax.optimization_barrier((received, keep, send))
    result = ffn(received.reshape(EXPERTS * capacity, feat_width), w_gate, w_up, w_down)
    result, got = lax.optimization_barrier((result, swap(send, "zh", 3)))
    result = result.reshape(EXPERTS, capacity, feat_width)
    returned = lax.all_to_all(result, SHARD, split_axis=0, concat_axis=0, tiled=True)
    moe_out = pl.pallas_call(
        combine_kernel,
        in_specs=whole(3),
        out_specs=whole(1)[0],
        out_shape=jax.ShapeDtypeStruct((tok_rows, feat_width), bf16),
        compiler_params=params(),
        name="combine",
    )(routes_t, weight_t, returned.reshape(EXPERTS * capacity, feat_width))
    block = outer_mean(keep, send, got)
    momentum_next, local_next, moe_out = outer_finish(moe_out, at, block, global_params, momentum, local_params)
    return (moe_out, momentum_next, local_next)


def solution(mesh):
    fine = Mesh(mesh.devices.reshape(4, 4, 2, 4, 2), REP + SHARD)
    in_specs = (
        P(REP + SHARD, None),
        P(REP + SHARD, None),
        P(REP + SHARD, None),
        P(SHARD, None, None),
        P(SHARD, None, None),
        P(SHARD, None, None),
        P(REP, SHARD, None),
        P(SHARD, None),
        P(SHARD, REP),
        P(REP, SHARD, None),
    )
    out_specs = (P(REP + SHARD, None), P(SHARD, REP), P(REP, SHARD, None))
    return jax.shard_map(local, mesh=fine, in_specs=in_specs, out_specs=out_specs, check_vma=False)
```

```python
import jax
import jax.numpy as jnp
from jax import lax
from jax.experimental import pallas as pl
from jax.experimental.pallas import tpu as pltpu
from jax.sharding import Mesh
from jax.sharding import PartitionSpec as P

f32 = jnp.float32
bf16 = jnp.bfloat16

outer_momentum = 0.9
outer_rate = 0.7
merge_weight = 0.5
clip_epsilon = 1e-06

EXPERTS = 8
REP = ("zh", "y", "c")
SHARD = ("x", "zl")
VMEM_LIMIT = 8 * 1024 * 1024
FFN_LIMIT = 52 * 1000000
DISPATCH_LIMIT = 58 * 1024 * 1024


def params(**more):
    return pltpu.CompilerParams(vmem_limit_bytes=VMEM_LIMIT, **more)


def whole(count):
    return [pl.BlockSpec(memory_space=pltpu.VMEM)] * count


def slots(routes, tokens, capacity):
    ids = lax.broadcasted_iota(jnp.int32, (EXPERTS, tokens), 0)
    named = jnp.logical_or(routes[0:1, :] == ids, routes[1:2, :] == ids)
    before = lax.broadcasted_iota(jnp.int32, (tokens, tokens), 0) < lax.broadcasted_iota(
        jnp.int32, (tokens, tokens), 1
    )
    place = jnp.dot(
        named.astype(f32).astype(bf16), before.astype(f32).astype(bf16), preferred_element_type=f32
    )
    return jnp.where(named, place.astype(jnp.int32), capacity)


def dispatch_kernel(routes_hbm, tokens_hbm, out_hbm, routes_ref, tokens_ref, out_ref, sems):
    tokens = tokens_ref.shape[0]
    capacity = out_ref.shape[1]
    width = 512
    parts = [pl.ds(j * width, width) for j in range(tokens_ref.shape[1] // width)]
    first = pltpu.make_async_copy(routes_hbm, routes_ref, sems.at[0])
    first.start()
    reads = [
        pltpu.make_async_copy(tokens_hbm.at[:, cols], tokens_ref.at[:, cols], sems.at[1 + j])
        for j, cols in enumerate(parts)
    ]
    for copy in reads:
        copy.start()
    first.wait()
    place = slots(routes_ref[...], tokens, capacity)
    row = lax.broadcasted_iota(jnp.int32, (capacity, tokens), 0)
    table = jnp.concatenate(
        [(row == place[e : e + 1, :]).astype(f32) for e in range(EXPERTS)], axis=0
    ).astype(bf16)
    writes = []
    for j, cols in enumerate(parts):
        reads[j].wait()
        part = jnp.dot(table, tokens_ref[:, cols], preferred_element_type=f32).astype(bf16)
        out_ref[:, :, cols] = part.reshape(EXPERTS, capacity, width)
        writes.append(
            pltpu.make_async_copy(out_ref.at[:, :, cols], out_hbm.at[:, :, cols], sems.at[1 + len(parts) + j])
        )
        writes[-1].start()
    for copy in writes:
        copy.wait()


def combine_kernel(table_ref, rows_ref, out_ref):
    tokens = table_ref.shape[1]
    capacity = rows_ref.shape[0] // EXPERTS
    routes = table_ref[0:2].astype(jnp.int32)
    place = slots(routes, tokens, capacity)
    row = lax.broadcasted_iota(jnp.int32, (capacity, tokens), 0)
    parts = []
    for e in range(EXPERTS):
        weight = jnp.where(routes[0:1, :] == e, table_ref[2:3, :], table_ref[3:4, :])
        parts.append(jnp.where(row == place[e : e + 1, :], weight, 0.0))
    table = jnp.concatenate(parts, axis=0).T
    high = table.astype(bf16)
    low = (table - high.astype(f32)).astype(bf16)
    width = 512
    for j in range(out_ref.shape[1] // width):
        cols = pl.ds(j * width, width)
        rows = rows_ref[:, cols]
        out_ref[:, cols] = (
            jnp.dot(high, rows, preferred_element_type=f32)
            + jnp.dot(low, rows, preferred_element_type=f32)
        ).astype(bf16)


def ffn_kernel(
    x_ref, gate_hbm, up_hbm, down_hbm, out_hbm, gate_ref, up_ref, down_ref, gated_ref, hidden_ref, out_ref, sems
):
    block, wide = 256, 512
    width, hidden = gate_ref.shape
    half, count = width // 2, hidden // block
    copies = []
    for hbm, ref in ((gate_hbm, gate_ref), (up_hbm, up_ref)):
        for i in range(2):
            rows = pl.ds(i * half, half)
            copies.append(pltpu.make_async_copy(hbm.at[0, rows], ref.at[rows], sems.at[len(copies)]))
    copies.append(pltpu.make_async_copy(down_hbm.at[0], down_ref, sems.at[4]))
    for copy in copies:
        copy.start()
    for i in range(2):
        rows = pl.ds(i * half, half)
        copies[i].wait()
        for n in range(count):
            cols = pl.ds(n * block, block)
            part = jnp.dot(x_ref[:, rows], gate_ref[rows, cols], preferred_element_type=f32)
            gated_ref[:, cols] = part if i == 0 else gated_ref[:, cols] + part
    copies[2].wait()
    copies[3].wait()
    for n in range(count):
        cols = pl.ds(n * block, block)
        up = jnp.dot(x_ref[...], up_ref[:, cols], preferred_element_type=f32)
        gate = gated_ref[:, cols]
        hidden_ref[:, cols] = (gate / (1.0 + jnp.exp(-gate)) * up).astype(bf16)
    copies[4].wait()
    results = []
    for n in range(width // wide):
        cols = pl.ds(n * wide, wide)
        out_ref[:, cols] = jnp.dot(
            hidden_ref[...], down_ref[:, cols], preferred_element_type=f32
        ).astype(bf16)
        results.append(pltpu.make_async_copy(out_ref.at[:, cols], out_hbm.at[:, cols], sems.at[5 + n]))
        results[-1].start()
    for copy in results:
        copy.wait()


def ffn(x, w_gate, w_up, w_down):
    rows, width = x.shape
    hidden = w_gate.shape[2]
    anywhere = pl.BlockSpec(memory_space=pl.ANY)
    return pl.pallas_call(
        ffn_kernel,
        in_specs=whole(1) + [anywhere] * 3,
        out_specs=anywhere,
        out_shape=jax.ShapeDtypeStruct((rows, width), bf16),
        scratch_shapes=[
            pltpu.VMEM((width, hidden), bf16),
            pltpu.VMEM((width, hidden), bf16),
            pltpu.VMEM((hidden, width), bf16),
            pltpu.VMEM((rows, hidden), f32),
            pltpu.VMEM((rows, hidden), bf16),
            pltpu.VMEM((rows, width), bf16),
            pltpu.SemaphoreType.DMA((5 + width // 512,)),
        ],
        compiler_params=pltpu.CompilerParams(vmem_limit_bytes=FFN_LIMIT),
        cost_estimate=pl.CostEstimate(
            flops=6 * rows * width * hidden,
            bytes_accessed=6 * width * hidden + 4 * rows * width,
            transcendentals=rows * hidden,
        ),
        name="expert_ffn",
    )(x, w_gate, w_up, w_down)


def halve_first_kernel(at_ref, own_ref, got_ref, keep_ref, send_ref):
    core, bit = at_ref[0], at_ref[1]
    half, width = got_ref.shape[1], keep_ref.shape[1]
    for ref, which in ((send_ref, 1 - bit), (keep_ref, bit)):
        mine = own_ref[0, :, pl.ds(pl.multiple_of(core * half + which * width, width), width)]
        other = got_ref[:, pl.ds(pl.multiple_of(which * width, width), width)]
        ref[...] = (mine + other).astype(ref.dtype)


def halve_kernel(at_ref, own_ref, got_ref, keep_ref, send_ref):
    bit, width = at_ref[2], keep_ref.shape[1]
    for ref, which in ((send_ref, 1 - bit), (keep_ref, bit)):
        cols = pl.ds(pl.multiple_of(which * width, width), width)
        ref[...] = (own_ref[:, cols] + got_ref[:, cols].astype(f32)).astype(ref.dtype)


def add_z_first_kernel(own_ref, got_ref, mom_ref, keep_ref, send_ref):
    rows = send_ref.shape[1]
    total = own_ref[...] + got_ref[...].astype(f32)
    for p in range(4):
        keep_ref[p] = total[(p & 1) * rows : (p & 1) * rows + rows, (p >> 1) * 128 : (p >> 1) * 128 + 128]
    send_ref[0:4] = keep_ref[...].astype(bf16)
    send_ref[4] = mom_ref[...].astype(bf16)


def add_z_kernel(own_ref, sent_ref, got_ref, keep_ref, send_ref):
    total = own_ref[...] + got_ref[0:4].astype(f32)
    keep_ref[...] = total
    send_ref[0:4] = total.astype(bf16)
    send_ref[4] = sent_ref[4]
    send_ref[5] = got_ref[4]


def mean_kernel(replicas, own_ref, sent_ref, got_ref, out_ref):
    total = own_ref[...] + got_ref[0:4].astype(f32)
    out_ref[0, 0:4] = (total * (1.0 / replicas)).astype(bf16)
    out_ref[0, 4:6] = sent_ref[4:6]
    out_ref[0, 6:8] = got_ref[4:6]


def square_kernel(a_ref, b_ref, out_ref):
    total = jnp.zeros(out_ref.shape, f32)
    step = out_ref.shape[0]
    for ref in (a_ref, b_ref):
        for j in range(4):
            for k in range(4):
                block = ref[j, k].astype(f32)
                block = block * block
                for i in range(block.shape[0] // step):
                    total += block[i * step : i * step + step]
    out_ref[...] = total


def quarter_of(y):
    return ((y & 1) ^ (y >> 1)) * 2 + (y >> 1)


def outer_kernel(entries, at_ref, near_s, far_s, near_ref, far_ref, params_ref, local_ref, mom_ref, next_ref, mom_out, scratch):
    core, quarter, zh, rep = at_ref[0], at_ref[3], at_ref[4], at_ref[5]
    squares = near_s[...] + far_s[...]
    squares = jnp.sum(jnp.sum(squares, axis=1, keepdims=True), axis=0, keepdims=True)
    clip = jnp.minimum(1.0, lax.rsqrt(squares * (1.0 / entries) + clip_epsilon))

    def delta(side, piece, slot):
        j = jnp.bitwise_xor(piece, quarter)
        return jnp.where(
            core == side, near_ref[j, slot].astype(f32), far_ref[j, slot].astype(f32)
        )

    for cb in range(16):
        j = jnp.bitwise_xor(quarter_of(cb & 3), quarter)
        apart = jnp.bitwise_xor(zh, cb >> 2)
        high = jnp.right_shift(apart, 1)
        slot = 4 + high * 2 + jnp.bitwise_xor(jnp.bitwise_and(apart, 1), high)
        near, far = near_ref[j, slot].astype(f32), far_ref[j, slot].astype(f32)
        m0, m1 = jnp.where(core == 0, near, far), jnp.where(core == 0, far, near)
        for h in range(2):
            rows, cols = pl.ds(h * 48, 48), pl.ds(cb * 128, 128)
            mom = jnp.concatenate([m0[:, h * 64 : h * 64 + 64], m1[:, h * 64 : h * 64 + 64]], axis=1)
            clipped = clip * delta(cb >> 3, (cb >> 1) & 3, (cb & 1) * 2 + h)
            after = outer_momentum * mom + clipped
            outer = params_ref[rows, cols] - outer_rate * (outer_momentum * after + clipped)
            local = local_ref[0, rows, cols].astype(f32)
            next_ref[0, rows, cols] = (merge_weight * local + (1.0 - merge_weight) * outer).astype(bf16)
    cb = jnp.right_shift(rep, 1)
    side, piece = jnp.right_shift(cb, 3), jnp.bitwise_and(jnp.right_shift(cb, 1), 3)
    scratch[...] = jnp.zeros_like(scratch)
    for h in range(2):
        scratch[h * 48 : h * 48 + 48, :] = delta(side, piece, jnp.bitwise_and(cb, 1) * 2 + h)
    scratch[...] = scratch[...].T
    start = pl.multiple_of(core * 64, 64)
    mom_out[...] = outer_momentum * mom_ref[...] + clip * scratch[pl.ds(start, 64), 0:96]


def smem():
    return pl.BlockSpec(memory_space=pltpu.SMEM)


def swap(value, axis, bits):
    size = lax.axis_size(axis)
    return lax.ppermute(value, axis, [(i, i ^ bits) for i in range(size)])


def outer_sum(pseudo_grad, momentum, routes_t, weight_t):
    rows, width = pseudo_grad.shape[1:]
    core, y, zh = lax.axis_index("c"), lax.axis_index("y"), lax.axis_index("zh")
    rep = (zh * 4 + y) * 2 + core
    first, second = (y & 1) ^ (y >> 1), y >> 1
    at = jnp.stack([core, first, second, first * 2 + second, zh, rep]).astype(jnp.int32)
    half = width // 2
    got = swap(lax.dynamic_slice_in_dim(pseudo_grad[0], (1 - core) * half, half, 1), "c", 1)
    keep, send = pl.pallas_call(
        halve_first_kernel,
        in_specs=[smem()] + whole(2),
        out_specs=whole(2),
        out_shape=[jax.ShapeDtypeStruct((rows, half // 2), t) for t in (f32, bf16)],
        compiler_params=params(),
        name="delta_halve_first",
    )(at, pseudo_grad, got)
    got = swap(send, "y", 1)
    keep, send = pl.pallas_call(
        halve_kernel,
        in_specs=[smem()] + whole(2),
        out_specs=whole(2),
        out_shape=[jax.ShapeDtypeStruct((rows, half // 4), t) for t in (f32, bf16)],
        compiler_params=params(),
        name="delta_halve",
    )(at, keep, got)
    got = swap(send, "y", 3)
    got, routes_t, weight_t = lax.optimization_barrier((got, routes_t, weight_t))
    table = jnp.concatenate([routes_t.astype(f32), weight_t], axis=0)
    part = (rows // 2, half // 8)
    mom_block = jnp.concatenate([momentum[: rows // 2], momentum[rows // 2 :]], axis=1)
    keep, send = pl.pallas_call(
        add_z_first_kernel,
        in_specs=whole(3),
        out_specs=whole(2),
        out_shape=[jax.ShapeDtypeStruct((4,) + part, f32), jax.ShapeDtypeStruct((5,) + part, bf16)],
        compiler_params=params(),
        name="delta_add_z_first",
    )(keep, got, mom_block)
    got = swap(send, "zh", 1)
    keep, send = pl.pallas_call(
        add_z_kernel,
        in_specs=whole(3),
        out_specs=whole(2),
        out_shape=[jax.ShapeDtypeStruct((4,) + part, f32), jax.ShapeDtypeStruct((6,) + part, bf16)],
        compiler_params=params(),
        name="delta_add_z",
    )(keep, send, got)
    return at, keep, send, table


def outer_mean(keep, send, got):
    part = keep.shape[1:]
    return pl.pallas_call(
        lambda *refs: mean_kernel(32, *refs),
        in_specs=whole(3),
        out_specs=whole(1)[0],
        out_shape=jax.ShapeDtypeStruct((1, 8) + part, bf16),
        compiler_params=params(),
        name="delta_mean",
    )(keep, send, got)


def outer_finish(moe_out, at, block, global_params, momentum, local_params):
    rows, width = global_params.shape
    block = jnp.concatenate([block, swap(block, "y", 3)], axis=0)
    block = jnp.concatenate([block, swap(block, "y", 1)], axis=0)
    far = swap(block, "c", 1)
    squares = pl.pallas_call(
        square_kernel,
        in_specs=whole(2),
        out_specs=whole(1)[0],
        out_shape=jax.ShapeDtypeStruct((8, 128), f32),
        compiler_params=params(),
        name="delta_squares",
    )(block, far)
    squares = squares + lax.ppermute(
        squares, ("zh", "zl"), [(z, (z + 1 if z % 2 else z - 1) % 8) for z in range(8)]
    )
    squares = squares + swap(squares, "x", 1)
    entries = float(rows * 8 * width)
    apart = swap(squares, "x", 3)
    apart, moe_out = lax.optimization_barrier((apart, moe_out))
    local_next, momentum_next = pl.pallas_call(
        lambda *refs: outer_kernel(entries, *refs),
        in_specs=[smem()] + whole(7),
        out_specs=whole(2),
        out_shape=[
            jax.ShapeDtypeStruct((1, rows, width), bf16),
            jax.ShapeDtypeStruct((momentum.shape[1], rows), f32),
        ],
        scratch_shapes=[pltpu.VMEM((128, 128), f32)],
        compiler_params=params(),
        name="outer_update",
    )(at, squares, apart, block, far, global_params, local_params, momentum.T)
    return momentum_next.T, local_next, moe_out


def local(
    tokens, routes, route_weight, w_gate, w_up, w_down, pseudo_grad, global_params, momentum, local_params
):
    tok_rows, feat_width = tokens.shape
    capacity = tok_rows * 3 // 8
    routes_t, weight_t = routes.T, route_weight.T
    outgoing = pl.pallas_call(
        dispatch_kernel,
        in_specs=[pl.BlockSpec(memory_space=pl.ANY)] * 2,
        out_specs=pl.BlockSpec(memory_space=pl.ANY),
        out_shape=jax.ShapeDtypeStruct((EXPERTS, capacity, feat_width), bf16),
        scratch_shapes=[
            pltpu.VMEM(routes_t.shape, jnp.int32),
            pltpu.VMEM(tokens.shape, bf16),
            pltpu.VMEM((EXPERTS, capacity, feat_width), bf16),
            pltpu.SemaphoreType.DMA((1 + 2 * (feat_width // 512),)),
        ],
        compiler_params=pltpu.CompilerParams(vmem_limit_bytes=DISPATCH_LIMIT),
        name="dispatch",
    )(routes_t, tokens)
    at, keep, send, table = outer_sum(pseudo_grad, momentum, routes_t, weight_t)
    received = lax.all_to_all(outgoing, SHARD, split_axis=0, concat_axis=0, tiled=True)
    received, keep, send = lax.optimization_barrier((received, keep, send))
    result = ffn(received.reshape(EXPERTS * capacity, feat_width), w_gate, w_up, w_down)
    result, got = lax.optimization_barrier((result, swap(send, "zh", 3)))
    result = result.reshape(EXPERTS, capacity, feat_width)
    returned = lax.all_to_all(result, SHARD, split_axis=0, concat_axis=0, tiled=True)
    moe_out = pl.pallas_call(
        combine_kernel,
        in_specs=whole(2),
        out_specs=whole(1)[0],
        out_shape=jax.ShapeDtypeStruct((tok_rows, feat_width), bf16),
        compiler_params=params(),
        name="combine",
    )(table, returned.reshape(EXPERTS * capacity, feat_width))
    block = outer_mean(keep, send, got)
    momentum_next, local_next, moe_out = outer_finish(moe_out, at, block, global_params, momentum, local_params)
    return (moe_out, momentum_next, local_next)


def solution(mesh):
    fine = Mesh(mesh.devices.reshape(4, 4, 2, 4, 2), REP + SHARD)
    in_specs = (
        P(REP + SHARD, None),
        P(REP + SHARD, None),
        P(REP + SHARD, None),
        P(SHARD, None, None),
        P(SHARD, None, None),
        P(SHARD, None, None),
        P(REP, SHARD, None),
        P(SHARD, None),
        P(SHARD, REP),
        P(REP, SHARD, None),
    )
    out_specs = (P(REP + SHARD, None), P(SHARD, REP), P(REP, SHARD, None))
    return jax.shard_map(local, mesh=fine, in_specs=in_specs, out_specs=out_specs, check_vma=False)
```

```python
import jax
import jax.numpy as jnp
from jax import lax
from jax.experimental import pallas as pl
from jax.experimental.pallas import tpu as pltpu
from jax.sharding import Mesh
from jax.sharding import PartitionSpec as P

f32 = jnp.float32
bf16 = jnp.bfloat16

outer_momentum = 0.9
outer_rate = 0.7
merge_weight = 0.5
clip_epsilon = 1e-06

EXPERTS = 8
REP = ("zh", "y", "c")
SHARD = ("x", "zl")
VMEM_LIMIT = 8 * 1024 * 1024
FFN_LIMIT = 52 * 1000000
DISPATCH_LIMIT = 58 * 1024 * 1024


def params(**more):
    return pltpu.CompilerParams(vmem_limit_bytes=VMEM_LIMIT, **more)


def whole(count):
    return [pl.BlockSpec(memory_space=pltpu.VMEM)] * count


def slots(routes, tokens, capacity):
    ids = lax.broadcasted_iota(jnp.int32, (EXPERTS, tokens), 0)
    named = jnp.logical_or(routes[0:1, :] == ids, routes[1:2, :] == ids)
    before = lax.broadcasted_iota(jnp.int32, (tokens, tokens), 0) < lax.broadcasted_iota(
        jnp.int32, (tokens, tokens), 1
    )
    place = jnp.dot(
        named.astype(f32).astype(bf16), before.astype(f32).astype(bf16), preferred_element_type=f32
    )
    return jnp.where(named, place.astype(jnp.int32), capacity)


def dispatch_kernel(routes_hbm, tokens_hbm, out_hbm, routes_ref, tokens_ref, out_ref, sems):
    tokens = tokens_ref.shape[0]
    capacity = out_ref.shape[1]
    width = 512
    parts = [pl.ds(j * width, width) for j in range(tokens_ref.shape[1] // width)]
    first = pltpu.make_async_copy(routes_hbm, routes_ref, sems.at[0])
    first.start()
    reads = [
        pltpu.make_async_copy(tokens_hbm.at[:, cols], tokens_ref.at[:, cols], sems.at[1 + j])
        for j, cols in enumerate(parts)
    ]
    for copy in reads:
        copy.start()
    first.wait()
    place = slots(routes_ref[...], tokens, capacity)
    row = lax.broadcasted_iota(jnp.int32, (capacity, tokens), 0)
    table = jnp.concatenate(
        [(row == place[e : e + 1, :]).astype(f32) for e in range(EXPERTS)], axis=0
    ).astype(bf16)
    writes = []
    for j, cols in enumerate(parts):
        reads[j].wait()
        part = jnp.dot(table, tokens_ref[:, cols], preferred_element_type=f32).astype(bf16)
        out_ref[:, :, cols] = part.reshape(EXPERTS, capacity, width)
        writes.append(
            pltpu.make_async_copy(out_ref.at[:, :, cols], out_hbm.at[:, :, cols], sems.at[1 + len(parts) + j])
        )
        writes[-1].start()
    for copy in writes:
        copy.wait()


def combine_kernel(table_ref, rows_ref, out_ref):
    tokens = table_ref.shape[1]
    capacity = rows_ref.shape[0] // EXPERTS
    routes = table_ref[0:2].astype(jnp.int32)
    place = slots(routes, tokens, capacity)
    row = lax.broadcasted_iota(jnp.int32, (capacity, tokens), 0)
    parts = []
    for e in range(EXPERTS):
        weight = jnp.where(routes[0:1, :] == e, table_ref[2:3, :], table_ref[3:4, :])
        parts.append(jnp.where(row == place[e : e + 1, :], weight, 0.0))
    table = jnp.concatenate(parts, axis=0).T
    high = table.astype(bf16)
    low = (table - high.astype(f32)).astype(bf16)
    width = 512
    for j in range(out_ref.shape[1] // width):
        cols = pl.ds(j * width, width)
        rows = rows_ref[:, cols]
        out_ref[:, cols] = (
            jnp.dot(high, rows, preferred_element_type=f32)
            + jnp.dot(low, rows, preferred_element_type=f32)
        ).astype(bf16)


def ffn_kernel(
    x_ref, gate_hbm, up_hbm, down_hbm, out_hbm, gate_ref, up_ref, down_ref, gated_ref, hidden_ref, out_ref, sems
):
    block, wide = 256, 512
    width, hidden = gate_ref.shape
    half, count = width // 2, hidden // block
    copies = []
    for hbm, ref in ((gate_hbm, gate_ref), (up_hbm, up_ref)):
        for i in range(2):
            rows = pl.ds(i * half, half)
            copies.append(pltpu.make_async_copy(hbm.at[0, rows], ref.at[rows], sems.at[len(copies)]))
    copies.append(pltpu.make_async_copy(down_hbm.at[0], down_ref, sems.at[4]))
    for copy in copies:
        copy.start()
    for i in range(2):
        rows = pl.ds(i * half, half)
        copies[i].wait()
        for n in range(count):
            cols = pl.ds(n * block, block)
            part = jnp.dot(x_ref[:, rows], gate_ref[rows, cols], preferred_element_type=f32)
            gated_ref[:, cols] = part if i == 0 else gated_ref[:, cols] + part
    copies[2].wait()
    copies[3].wait()
    for n in range(count):
        cols = pl.ds(n * block, block)
        up = jnp.dot(x_ref[...], up_ref[:, cols], preferred_element_type=f32)
        gate = gated_ref[:, cols]
        hidden_ref[:, cols] = (gate / (1.0 + jnp.exp(-gate)) * up).astype(bf16)
    copies[4].wait()
    results = []
    for n in range(width // wide):
        cols = pl.ds(n * wide, wide)
        out_ref[:, cols] = jnp.dot(
            hidden_ref[...], down_ref[:, cols], preferred_element_type=f32
        ).astype(bf16)
        results.append(pltpu.make_async_copy(out_ref.at[:, cols], out_hbm.at[:, cols], sems.at[5 + n]))
        results[-1].start()
    for copy in results:
        copy.wait()


def ffn(x, w_gate, w_up, w_down):
    rows, width = x.shape
    hidden = w_gate.shape[2]
    anywhere = pl.BlockSpec(memory_space=pl.ANY)
    return pl.pallas_call(
        ffn_kernel,
        in_specs=whole(1) + [anywhere] * 3,
        out_specs=anywhere,
        out_shape=jax.ShapeDtypeStruct((rows, width), bf16),
        scratch_shapes=[
            pltpu.VMEM((width, hidden), bf16),
            pltpu.VMEM((width, hidden), bf16),
            pltpu.VMEM((hidden, width), bf16),
            pltpu.VMEM((rows, hidden), f32),
            pltpu.VMEM((rows, hidden), bf16),
            pltpu.VMEM((rows, width), bf16),
            pltpu.SemaphoreType.DMA((5 + width // 512,)),
        ],
        compiler_params=pltpu.CompilerParams(vmem_limit_bytes=FFN_LIMIT),
        cost_estimate=pl.CostEstimate(
            flops=6 * rows * width * hidden,
            bytes_accessed=6 * width * hidden + 4 * rows * width,
            transcendentals=rows * hidden,
        ),
        name="expert_ffn",
    )(x, w_gate, w_up, w_down)


def halve_first_kernel(at_ref, own_ref, got_ref, keep_ref, send_ref):
    core, bit = at_ref[0], at_ref[1]
    half, width = got_ref.shape[1], keep_ref.shape[1]
    for ref, which in ((send_ref, 1 - bit), (keep_ref, bit)):
        mine = own_ref[0, :, pl.ds(pl.multiple_of(core * half + which * width, width), width)]
        other = got_ref[:, pl.ds(pl.multiple_of(which * width, width), width)]
        ref[...] = (mine + other).astype(ref.dtype)


def halve_kernel(at_ref, own_ref, got_ref, keep_ref, send_ref):
    bit, width = at_ref[2], keep_ref.shape[1]
    for ref, which in ((send_ref, 1 - bit), (keep_ref, bit)):
        cols = pl.ds(pl.multiple_of(which * width, width), width)
        ref[...] = (own_ref[:, cols] + got_ref[:, cols].astype(f32)).astype(ref.dtype)


def add_z_first_kernel(own_ref, got_ref, mom_ref, keep_ref, send_ref):
    rows = send_ref.shape[1]
    total = own_ref[...] + got_ref[...].astype(f32)
    for p in range(4):
        keep_ref[p] = total[(p & 1) * rows : (p & 1) * rows + rows, (p >> 1) * 128 : (p >> 1) * 128 + 128]
    send_ref[0:4] = keep_ref[...].astype(bf16)
    send_ref[4] = mom_ref[...].astype(bf16)


def add_z_kernel(own_ref, sent_ref, got_ref, keep_ref, send_ref):
    total = own_ref[...] + got_ref[0:4].astype(f32)
    keep_ref[...] = total
    send_ref[0:4] = total.astype(bf16)
    send_ref[4] = sent_ref[4]
    send_ref[5] = got_ref[4]


def mean_kernel(replicas, own_ref, sent_ref, got_ref, out_ref):
    total = own_ref[...] + got_ref[0:4].astype(f32)
    out_ref[0, 0:4] = (total * (1.0 / replicas)).astype(bf16)
    out_ref[0, 4:6] = sent_ref[4:6]
    out_ref[0, 6:8] = got_ref[4:6]


def square_kernel(a_ref, b_ref, out_ref):
    total = jnp.zeros(out_ref.shape, f32)
    step = out_ref.shape[0]
    for ref in (a_ref, b_ref):
        for j in range(4):
            for k in range(4):
                block = ref[j, k].astype(f32)
                block = block * block
                for i in range(block.shape[0] // step):
                    total += block[i * step : i * step + step]
    out_ref[...] = total


def quarter_of(y):
    return ((y & 1) ^ (y >> 1)) * 2 + (y >> 1)


def outer_kernel(entries, at_ref, near_s, far_s, near_ref, far_ref, params_ref, local_ref, mom_ref, next_ref, mom_out, scratch):
    core, quarter, zh, rep = at_ref[0], at_ref[3], at_ref[4], at_ref[5]
    squares = near_s[...] + far_s[...]
    squares = jnp.sum(jnp.sum(squares, axis=1, keepdims=True), axis=0, keepdims=True)
    clip = jnp.minimum(1.0, lax.rsqrt(squares * (1.0 / entries) + clip_epsilon))

    def delta(side, piece, slot):
        j = jnp.bitwise_xor(piece, quarter)
        return jnp.where(
            core == side, near_ref[j, slot].astype(f32), far_ref[j, slot].astype(f32)
        )

    for cb in range(16):
        j = jnp.bitwise_xor(quarter_of(cb & 3), quarter)
        apart = jnp.bitwise_xor(zh, cb >> 2)
        high = jnp.right_shift(apart, 1)
        slot = 4 + high * 2 + jnp.bitwise_xor(jnp.bitwise_and(apart, 1), high)
        near, far = near_ref[j, slot].astype(f32), far_ref[j, slot].astype(f32)
        m0, m1 = jnp.where(core == 0, near, far), jnp.where(core == 0, far, near)
        for h in range(2):
            rows, cols = pl.ds(h * 48, 48), pl.ds(cb * 128, 128)
            mom = jnp.concatenate([m0[:, h * 64 : h * 64 + 64], m1[:, h * 64 : h * 64 + 64]], axis=1)
            clipped = clip * delta(cb >> 3, (cb >> 1) & 3, (cb & 1) * 2 + h)
            after = outer_momentum * mom + clipped
            outer = params_ref[rows, cols] - outer_rate * (outer_momentum * after + clipped)
            local = local_ref[0, rows, cols].astype(f32)
            next_ref[0, rows, cols] = (merge_weight * local + (1.0 - merge_weight) * outer).astype(bf16)
    cb = jnp.right_shift(rep, 1)
    side, piece = jnp.right_shift(cb, 3), jnp.bitwise_and(jnp.right_shift(cb, 1), 3)
    scratch[...] = jnp.zeros_like(scratch)
    for h in range(2):
        scratch[h * 48 : h * 48 + 48, :] = delta(side, piece, jnp.bitwise_and(cb, 1) * 2 + h)
    scratch[...] = scratch[...].T
    start = pl.multiple_of(core * 64, 64)
    mom_out[...] = outer_momentum * mom_ref[...] + clip * scratch[pl.ds(start, 64), 0:96]


def smem():
    return pl.BlockSpec(memory_space=pltpu.SMEM)


def swap(value, axis, bits):
    size = lax.axis_size(axis)
    return lax.ppermute(value, axis, [(i, i ^ bits) for i in range(size)])


def outer_sum(pseudo_grad, momentum, routes_t, weight_t):
    rows, width = pseudo_grad.shape[1:]
    core, y, zh = lax.axis_index("c"), lax.axis_index("y"), lax.axis_index("zh")
    rep = (zh * 4 + y) * 2 + core
    first, second = (y & 1) ^ (y >> 1), y >> 1
    at = jnp.stack([core, first, second, first * 2 + second, zh, rep]).astype(jnp.int32)
    half = width // 2
    got = swap(lax.dynamic_slice_in_dim(pseudo_grad[0], (1 - core) * half, half, 1), "c", 1)
    keep, send = pl.pallas_call(
        halve_first_kernel,
        in_specs=[smem()] + whole(2),
        out_specs=whole(2),
        out_shape=[jax.ShapeDtypeStruct((rows, half // 2), t) for t in (f32, bf16)],
        compiler_params=params(),
        name="delta_halve_first",
    )(at, pseudo_grad, got)
    got = swap(send, "y", 1)
    keep, send = pl.pallas_call(
        halve_kernel,
        in_specs=[smem()] + whole(2),
        out_specs=whole(2),
        out_shape=[jax.ShapeDtypeStruct((rows, half // 4), t) for t in (f32, bf16)],
        compiler_params=params(),
        name="delta_halve",
    )(at, keep, got)
    got = swap(send, "y", 3)
    got, routes_t, weight_t = lax.optimization_barrier((got, routes_t, weight_t))
    table = jnp.concatenate([routes_t.astype(f32), weight_t], axis=0)
    part = (rows // 2, half // 8)
    mom_block = jnp.concatenate([momentum[: rows // 2], momentum[rows // 2 :]], axis=1)
    keep, send = pl.pallas_call(
        add_z_first_kernel,
        in_specs=whole(3),
        out_specs=whole(2),
        out_shape=[jax.ShapeDtypeStruct((4,) + part, f32), jax.ShapeDtypeStruct((5,) + part, bf16)],
        compiler_params=params(),
        name="delta_add_z_first",
    )(keep, got, mom_block)
    got = swap(send, "zh", 1)
    keep, send = pl.pallas_call(
        add_z_kernel,
        in_specs=whole(3),
        out_specs=whole(2),
        out_shape=[jax.ShapeDtypeStruct((4,) + part, f32), jax.ShapeDtypeStruct((6,) + part, bf16)],
        compiler_params=params(),
        name="delta_add_z",
    )(keep, send, got)
    return at, keep, send, table


def outer_mean(keep, send, got):
    part = keep.shape[1:]
    return pl.pallas_call(
        lambda *refs: mean_kernel(32, *refs),
        in_specs=whole(3),
        out_specs=whole(1)[0],
        out_shape=jax.ShapeDtypeStruct((1, 8) + part, bf16),
        compiler_params=params(),
        name="delta_mean",
    )(keep, send, got)


def outer_finish(moe_out, at, block, global_params, momentum, local_params):
    rows, width = global_params.shape
    block = jnp.concatenate([block, swap(block, "y", 3)], axis=0)
    block = jnp.concatenate([block, swap(block, "y", 1)], axis=0)
    far = swap(block, "c", 1)
    squares = pl.pallas_call(
        square_kernel,
        in_specs=whole(2),
        out_specs=whole(1)[0],
        out_shape=jax.ShapeDtypeStruct((8, 128), f32),
        compiler_params=params(),
        name="delta_squares",
    )(block, far)
    squares = squares + lax.ppermute(
        squares, ("zh", "zl"), [(z, (z + 1 if z % 2 else z - 1) % 8) for z in range(8)]
    )
    squares = squares + swap(squares, "x", 1)
    entries = float(rows * 8 * width)
    apart = swap(squares, "x", 3)
    apart, moe_out = lax.optimization_barrier((apart, moe_out))
    local_next, momentum_next = pl.pallas_call(
        lambda *refs: outer_kernel(entries, *refs),
        in_specs=[smem()] + whole(7),
        out_specs=whole(2),
        out_shape=[
            jax.ShapeDtypeStruct((1, rows, width), bf16),
            jax.ShapeDtypeStruct((momentum.shape[1], rows), f32),
        ],
        scratch_shapes=[pltpu.VMEM((128, 128), f32)],
        compiler_params=params(),
        name="outer_update",
    )(at, squares, apart, block, far, global_params, local_params, momentum.T)
    return momentum_next.T, local_next, moe_out


def local(
    tokens, routes, route_weight, w_gate, w_up, w_down, pseudo_grad, global_params, momentum, local_params
):
    tok_rows, feat_width = tokens.shape
    capacity = tok_rows * 3 // 8
    routes_t, weight_t = routes.T, route_weight.T
    outgoing = pl.pallas_call(
        dispatch_kernel,
        in_specs=[pl.BlockSpec(memory_space=pl.ANY)] * 2,
        out_specs=pl.BlockSpec(memory_space=pl.ANY),
        out_shape=jax.ShapeDtypeStruct((EXPERTS, capacity, feat_width), bf16),
        scratch_shapes=[
            pltpu.VMEM(routes_t.shape, jnp.int32),
            pltpu.VMEM(tokens.shape, bf16),
            pltpu.VMEM((EXPERTS, capacity, feat_width), bf16),
            pltpu.SemaphoreType.DMA((1 + 2 * (feat_width // 512),)),
        ],
        compiler_params=pltpu.CompilerParams(vmem_limit_bytes=DISPATCH_LIMIT),
        name="dispatch",
    )(routes_t, tokens)
    at, keep, send, table = outer_sum(pseudo_grad, momentum, routes_t, weight_t)
    received = lax.all_to_all(outgoing, SHARD, split_axis=0, concat_axis=0, tiled=True)
    received, keep, send = lax.optimization_barrier((received, keep, send))
    result = ffn(received.reshape(EXPERTS * capacity, feat_width), w_gate, w_up, w_down)
    result, send = lax.optimization_barrier((result, send))
    result, got = lax.optimization_barrier((result, swap(send, "zh", 3)))
    result = result.reshape(EXPERTS, capacity, feat_width)
    returned = lax.all_to_all(result, SHARD, split_axis=0, concat_axis=0, tiled=True)
    moe_out = pl.pallas_call(
        combine_kernel,
        in_specs=whole(2),
        out_specs=whole(1)[0],
        out_shape=jax.ShapeDtypeStruct((tok_rows, feat_width), bf16),
        compiler_params=params(),
        name="combine",
    )(table, returned.reshape(EXPERTS * capacity, feat_width))
    block = outer_mean(keep, send, got)
    momentum_next, local_next, moe_out = outer_finish(moe_out, at, block, global_params, momentum, local_params)
    return (moe_out, momentum_next, local_next)


def solution(mesh):
    fine = Mesh(mesh.devices.reshape(4, 4, 2, 4, 2), REP + SHARD)
    in_specs = (
        P(REP + SHARD, None),
        P(REP + SHARD, None),
        P(REP + SHARD, None),
        P(SHARD, None, None),
        P(SHARD, None, None),
        P(SHARD, None, None),
        P(REP, SHARD, None),
        P(SHARD, None),
        P(SHARD, REP),
        P(REP, SHARD, None),
    )
    out_specs = (P(REP + SHARD, None), P(SHARD, REP), P(REP, SHARD, None))
    return jax.shard_map(local, mesh=fine, in_specs=in_specs, out_specs=out_specs, check_vma=False)
```

```python
import jax
import jax.numpy as jnp
from jax import lax
from jax.experimental import pallas as pl
from jax.experimental.pallas import tpu as pltpu
from jax.sharding import Mesh
from jax.sharding import PartitionSpec as P

f32 = jnp.float32
bf16 = jnp.bfloat16

outer_momentum = 0.9
outer_rate = 0.7
merge_weight = 0.5
clip_epsilon = 1e-06

EXPERTS = 8
REP = ("zh", "y", "c")
SHARD = ("x", "zl")
VMEM_LIMIT = 8 * 1024 * 1024
FFN_LIMIT = 52 * 1000000
DISPATCH_LIMIT = 58 * 1024 * 1024


def params(**more):
    return pltpu.CompilerParams(vmem_limit_bytes=VMEM_LIMIT, **more)


def whole(count):
    return [pl.BlockSpec(memory_space=pltpu.VMEM)] * count


def slots(routes, tokens, capacity):
    ids = lax.broadcasted_iota(jnp.int32, (EXPERTS, tokens), 0)
    named = jnp.logical_or(routes[0:1, :] == ids, routes[1:2, :] == ids)
    before = lax.broadcasted_iota(jnp.int32, (tokens, tokens), 0) < lax.broadcasted_iota(
        jnp.int32, (tokens, tokens), 1
    )
    place = jnp.dot(
        named.astype(f32).astype(bf16), before.astype(f32).astype(bf16), preferred_element_type=f32
    )
    return jnp.where(named, place.astype(jnp.int32), capacity)


def dispatch_kernel(routes_hbm, tokens_hbm, out_hbm, routes_ref, tokens_ref, out_ref, sems):
    tokens = tokens_ref.shape[0]
    capacity = out_ref.shape[1]
    width = 512
    parts = [pl.ds(j * width, width) for j in range(tokens_ref.shape[1] // width)]
    first = pltpu.make_async_copy(routes_hbm, routes_ref, sems.at[0])
    first.start()
    reads = [
        pltpu.make_async_copy(tokens_hbm.at[:, cols], tokens_ref.at[:, cols], sems.at[1 + j])
        for j, cols in enumerate(parts)
    ]
    for copy in reads:
        copy.start()
    first.wait()
    place = slots(routes_ref[...], tokens, capacity)
    row = lax.broadcasted_iota(jnp.int32, (capacity, tokens), 0)
    table = jnp.concatenate(
        [(row == place[e : e + 1, :]).astype(f32) for e in range(EXPERTS)], axis=0
    ).astype(bf16)
    writes = []
    for j, cols in enumerate(parts):
        reads[j].wait()
        part = jnp.dot(table, tokens_ref[:, cols], preferred_element_type=f32).astype(bf16)
        out_ref[:, :, cols] = part.reshape(EXPERTS, capacity, width)
        writes.append(
            pltpu.make_async_copy(out_ref.at[:, :, cols], out_hbm.at[:, :, cols], sems.at[1 + len(parts) + j])
        )
        writes[-1].start()
    for copy in writes:
        copy.wait()


def combine_kernel(table_ref, rows_ref, out_ref):
    tokens = table_ref.shape[1]
    capacity = rows_ref.shape[0] // EXPERTS
    routes = table_ref[0:2].astype(jnp.int32)
    place = slots(routes, tokens, capacity)
    row = lax.broadcasted_iota(jnp.int32, (capacity, tokens), 0)
    parts = []
    for e in range(EXPERTS):
        weight = jnp.where(routes[0:1, :] == e, table_ref[2:3, :], table_ref[3:4, :])
        parts.append(jnp.where(row == place[e : e + 1, :], weight, 0.0))
    table = jnp.concatenate(parts, axis=0).T
    high = table.astype(bf16)
    low = (table - high.astype(f32)).astype(bf16)
    width = 512
    for j in range(out_ref.shape[1] // width):
        cols = pl.ds(j * width, width)
        rows = rows_ref[:, cols]
        out_ref[:, cols] = (
            jnp.dot(high, rows, preferred_element_type=f32)
            + jnp.dot(low, rows, preferred_element_type=f32)
        ).astype(bf16)


def ffn_kernel(
    x_ref, gate_hbm, up_hbm, down_hbm, out_hbm, gate_ref, up_ref, down_ref, gated_ref, hidden_ref, out_ref, sems
):
    block, wide = 256, 512
    width, hidden = gate_ref.shape
    half, count = width // 2, hidden // block
    copies = []
    for hbm, ref in ((gate_hbm, gate_ref), (up_hbm, up_ref)):
        for i in range(2):
            rows = pl.ds(i * half, half)
            copies.append(pltpu.make_async_copy(hbm.at[0, rows], ref.at[rows], sems.at[len(copies)]))
    copies.append(pltpu.make_async_copy(down_hbm.at[0], down_ref, sems.at[4]))
    copies[0].start()
    copies[1].start()
    for i in range(2):
        rows = pl.ds(i * half, half)
        copies[i].wait()
        for copy in copies[2:4] if i == 0 else copies[4:5]:
            copy.start()
        for n in range(count):
            cols = pl.ds(n * block, block)
            part = jnp.dot(x_ref[:, rows], gate_ref[rows, cols], preferred_element_type=f32)
            gated_ref[:, cols] = part if i == 0 else gated_ref[:, cols] + part
    copies[2].wait()
    copies[3].wait()
    for n in range(count):
        cols = pl.ds(n * block, block)
        up = jnp.dot(x_ref[...], up_ref[:, cols], preferred_element_type=f32)
        gate = gated_ref[:, cols]
        hidden_ref[:, cols] = (gate / (1.0 + jnp.exp(-gate)) * up).astype(bf16)
    copies[4].wait()
    results = []
    for n in range(width // wide):
        cols = pl.ds(n * wide, wide)
        out_ref[:, cols] = jnp.dot(
            hidden_ref[...], down_ref[:, cols], preferred_element_type=f32
        ).astype(bf16)
        results.append(pltpu.make_async_copy(out_ref.at[:, cols], out_hbm.at[:, cols], sems.at[5 + n]))
        results[-1].start()
    for copy in results:
        copy.wait()


def ffn(x, w_gate, w_up, w_down):
    rows, width = x.shape
    hidden = w_gate.shape[2]
    anywhere = pl.BlockSpec(memory_space=pl.ANY)
    return pl.pallas_call(
        ffn_kernel,
        in_specs=whole(1) + [anywhere] * 3,
        out_specs=anywhere,
        out_shape=jax.ShapeDtypeStruct((rows, width), bf16),
        scratch_shapes=[
            pltpu.VMEM((width, hidden), bf16),
            pltpu.VMEM((width, hidden), bf16),
            pltpu.VMEM((hidden, width), bf16),
            pltpu.VMEM((rows, hidden), f32),
            pltpu.VMEM((rows, hidden), bf16),
            pltpu.VMEM((rows, width), bf16),
            pltpu.SemaphoreType.DMA((5 + width // 512,)),
        ],
        compiler_params=pltpu.CompilerParams(vmem_limit_bytes=FFN_LIMIT),
        cost_estimate=pl.CostEstimate(
            flops=6 * rows * width * hidden,
            bytes_accessed=6 * width * hidden + 4 * rows * width,
            transcendentals=rows * hidden,
        ),
        name="expert_ffn",
    )(x, w_gate, w_up, w_down)


def halve_first_kernel(at_ref, own_ref, got_ref, keep_ref, send_ref):
    core, bit = at_ref[0], at_ref[1]
    half, width = got_ref.shape[1], keep_ref.shape[1]
    for ref, which in ((send_ref, 1 - bit), (keep_ref, bit)):
        mine = own_ref[0, :, pl.ds(pl.multiple_of(core * half + which * width, width), width)]
        other = got_ref[:, pl.ds(pl.multiple_of(which * width, width), width)]
        ref[...] = (mine + other).astype(ref.dtype)


def halve_kernel(at_ref, own_ref, got_ref, keep_ref, send_ref):
    bit, width = at_ref[2], keep_ref.shape[1]
    for ref, which in ((send_ref, 1 - bit), (keep_ref, bit)):
        cols = pl.ds(pl.multiple_of(which * width, width), width)
        ref[...] = (own_ref[:, cols] + got_ref[:, cols].astype(f32)).astype(ref.dtype)


def add_z_first_kernel(own_ref, got_ref, mom_ref, keep_ref, send_ref):
    rows = send_ref.shape[1]
    total = own_ref[...] + got_ref[...].astype(f32)
    for p in range(4):
        keep_ref[p] = total[(p & 1) * rows : (p & 1) * rows + rows, (p >> 1) * 128 : (p >> 1) * 128 + 128]
    send_ref[0:4] = keep_ref[...].astype(bf16)
    send_ref[4] = mom_ref[...].astype(bf16)


def add_z_kernel(own_ref, sent_ref, got_ref, keep_ref, send_ref):
    total = own_ref[...] + got_ref[0:4].astype(f32)
    keep_ref[...] = total
    send_ref[0:4] = total.astype(bf16)
    send_ref[4] = sent_ref[4]
    send_ref[5] = got_ref[4]


def mean_kernel(replicas, own_ref, sent_ref, got_ref, out_ref):
    total = own_ref[...] + got_ref[0:4].astype(f32)
    out_ref[0, 0:4] = (total * (1.0 / replicas)).astype(bf16)
    out_ref[0, 4:6] = sent_ref[4:6]
    out_ref[0, 6:8] = got_ref[4:6]


def square_kernel(a_ref, b_ref, out_ref):
    total = jnp.zeros(out_ref.shape, f32)
    step = out_ref.shape[0]
    for ref in (a_ref, b_ref):
        for j in range(4):
            for k in range(4):
                block = ref[j, k].astype(f32)
                block = block * block
                for i in range(block.shape[0] // step):
                    total += block[i * step : i * step + step]
    out_ref[...] = total


def quarter_of(y):
    return ((y & 1) ^ (y >> 1)) * 2 + (y >> 1)


def outer_kernel(entries, at_ref, near_s, far_s, near_ref, far_ref, params_ref, local_ref, mom_ref, next_ref, mom_out, scratch):
    core, quarter, zh, rep = at_ref[0], at_ref[3], at_ref[4], at_ref[5]
    squares = near_s[...] + far_s[...]
    squares = jnp.sum(jnp.sum(squares, axis=1, keepdims=True), axis=0, keepdims=True)
    clip = jnp.minimum(1.0, lax.rsqrt(squares * (1.0 / entries) + clip_epsilon))

    def delta(side, piece, slot):
        j = jnp.bitwise_xor(piece, quarter)
        return jnp.where(
            core == side, near_ref[j, slot].astype(f32), far_ref[j, slot].astype(f32)
        )

    for cb in range(16):
        j = jnp.bitwise_xor(quarter_of(cb & 3), quarter)
        apart = jnp.bitwise_xor(zh, cb >> 2)
        high = jnp.right_shift(apart, 1)
        slot = 4 + high * 2 + jnp.bitwise_xor(jnp.bitwise_and(apart, 1), high)
        near, far = near_ref[j, slot].astype(f32), far_ref[j, slot].astype(f32)
        m0, m1 = jnp.where(core == 0, near, far), jnp.where(core == 0, far, near)
        for h in range(2):
            rows, cols = pl.ds(h * 48, 48), pl.ds(cb * 128, 128)
            mom = jnp.concatenate([m0[:, h * 64 : h * 64 + 64], m1[:, h * 64 : h * 64 + 64]], axis=1)
            clipped = clip * delta(cb >> 3, (cb >> 1) & 3, (cb & 1) * 2 + h)
            after = outer_momentum * mom + clipped
            outer = params_ref[rows, cols] - outer_rate * (outer_momentum * after + clipped)
            local = local_ref[0, rows, cols].astype(f32)
            next_ref[0, rows, cols] = (merge_weight * local + (1.0 - merge_weight) * outer).astype(bf16)
    cb = jnp.right_shift(rep, 1)
    side, piece = jnp.right_shift(cb, 3), jnp.bitwise_and(jnp.right_shift(cb, 1), 3)
    scratch[...] = jnp.zeros_like(scratch)
    for h in range(2):
        scratch[h * 48 : h * 48 + 48, :] = delta(side, piece, jnp.bitwise_and(cb, 1) * 2 + h)
    scratch[...] = scratch[...].T
    start = pl.multiple_of(core * 64, 64)
    mom_out[...] = outer_momentum * mom_ref[...] + clip * scratch[pl.ds(start, 64), 0:96]


def smem():
    return pl.BlockSpec(memory_space=pltpu.SMEM)


def swap(value, axis, bits):
    size = lax.axis_size(axis)
    return lax.ppermute(value, axis, [(i, i ^ bits) for i in range(size)])


def outer_sum(pseudo_grad, momentum, routes_t, weight_t):
    rows, width = pseudo_grad.shape[1:]
    core, y, zh = lax.axis_index("c"), lax.axis_index("y"), lax.axis_index("zh")
    rep = (zh * 4 + y) * 2 + core
    first, second = (y & 1) ^ (y >> 1), y >> 1
    at = jnp.stack([core, first, second, first * 2 + second, zh, rep]).astype(jnp.int32)
    half = width // 2
    got = swap(lax.dynamic_slice_in_dim(pseudo_grad[0], (1 - core) * half, half, 1), "c", 1)
    keep, send = pl.pallas_call(
        halve_first_kernel,
        in_specs=[smem()] + whole(2),
        out_specs=whole(2),
        out_shape=[jax.ShapeDtypeStruct((rows, half // 2), t) for t in (f32, bf16)],
        compiler_params=params(),
        name="delta_halve_first",
    )(at, pseudo_grad, got)
    got = swap(send, "y", 1)
    keep, send = pl.pallas_call(
        halve_kernel,
        in_specs=[smem()] + whole(2),
        out_specs=whole(2),
        out_shape=[jax.ShapeDtypeStruct((rows, half // 4), t) for t in (f32, bf16)],
        compiler_params=params(),
        name="delta_halve",
    )(at, keep, got)
    got = swap(send, "y", 3)
    got, routes_t, weight_t = lax.optimization_barrier((got, routes_t, weight_t))
    table = jnp.concatenate([routes_t.astype(f32), weight_t], axis=0)
    part = (rows // 2, half // 8)
    mom_block = jnp.concatenate([momentum[: rows // 2], momentum[rows // 2 :]], axis=1)
    keep, send = pl.pallas_call(
        add_z_first_kernel,
        in_specs=whole(3),
        out_specs=whole(2),
        out_shape=[jax.ShapeDtypeStruct((4,) + part, f32), jax.ShapeDtypeStruct((5,) + part, bf16)],
        compiler_params=params(),
        name="delta_add_z_first",
    )(keep, got, mom_block)
    got = swap(send, "zh", 1)
    keep, send = pl.pallas_call(
        add_z_kernel,
        in_specs=whole(3),
        out_specs=whole(2),
        out_shape=[jax.ShapeDtypeStruct((4,) + part, f32), jax.ShapeDtypeStruct((6,) + part, bf16)],
        compiler_params=params(),
        name="delta_add_z",
    )(keep, send, got)
    return at, keep, send, table


def outer_mean(keep, send, got):
    part = keep.shape[1:]
    return pl.pallas_call(
        lambda *refs: mean_kernel(32, *refs),
        in_specs=whole(3),
        out_specs=whole(1)[0],
        out_shape=jax.ShapeDtypeStruct((1, 8) + part, bf16),
        compiler_params=params(),
        name="delta_mean",
    )(keep, send, got)


def outer_finish(moe_out, at, block, global_params, momentum, local_params):
    rows, width = global_params.shape
    block = jnp.concatenate([block, swap(block, "y", 3)], axis=0)
    block = jnp.concatenate([block, swap(block, "y", 1)], axis=0)
    far = swap(block, "c", 1)
    squares = pl.pallas_call(
        square_kernel,
        in_specs=whole(2),
        out_specs=whole(1)[0],
        out_shape=jax.ShapeDtypeStruct((8, 128), f32),
        compiler_params=params(),
        name="delta_squares",
    )(block, far)
    squares = squares + lax.ppermute(
        squares, ("zh", "zl"), [(z, (z + 1 if z % 2 else z - 1) % 8) for z in range(8)]
    )
    squares = squares + swap(squares, "x", 1)
    entries = float(rows * 8 * width)
    apart = swap(squares, "x", 3)
    apart, moe_out = lax.optimization_barrier((apart, moe_out))
    local_next, momentum_next = pl.pallas_call(
        lambda *refs: outer_kernel(entries, *refs),
        in_specs=[smem()] + whole(7),
        out_specs=whole(2),
        out_shape=[
            jax.ShapeDtypeStruct((1, rows, width), bf16),
            jax.ShapeDtypeStruct((momentum.shape[1], rows), f32),
        ],
        scratch_shapes=[pltpu.VMEM((128, 128), f32)],
        compiler_params=params(),
        name="outer_update",
    )(at, squares, apart, block, far, global_params, local_params, momentum.T)
    return momentum_next.T, local_next, moe_out


def local(
    tokens, routes, route_weight, w_gate, w_up, w_down, pseudo_grad, global_params, momentum, local_params
):
    tok_rows, feat_width = tokens.shape
    capacity = tok_rows * 3 // 8
    routes_t, weight_t = routes.T, route_weight.T
    outgoing = pl.pallas_call(
        dispatch_kernel,
        in_specs=[pl.BlockSpec(memory_space=pl.ANY)] * 2,
        out_specs=pl.BlockSpec(memory_space=pl.ANY),
        out_shape=jax.ShapeDtypeStruct((EXPERTS, capacity, feat_width), bf16),
        scratch_shapes=[
            pltpu.VMEM(routes_t.shape, jnp.int32),
            pltpu.VMEM(tokens.shape, bf16),
            pltpu.VMEM((EXPERTS, capacity, feat_width), bf16),
            pltpu.SemaphoreType.DMA((1 + 2 * (feat_width // 512),)),
        ],
        compiler_params=pltpu.CompilerParams(vmem_limit_bytes=DISPATCH_LIMIT),
        name="dispatch",
    )(routes_t, tokens)
    at, keep, send, table = outer_sum(pseudo_grad, momentum, routes_t, weight_t)
    received = lax.all_to_all(outgoing, SHARD, split_axis=0, concat_axis=0, tiled=True)
    received, keep, send = lax.optimization_barrier((received, keep, send))
    result = ffn(received.reshape(EXPERTS * capacity, feat_width), w_gate, w_up, w_down)
    result, got = lax.optimization_barrier((result, swap(send, "zh", 3)))
    result = result.reshape(EXPERTS, capacity, feat_width)
    returned = lax.all_to_all(result, SHARD, split_axis=0, concat_axis=0, tiled=True)
    moe_out = pl.pallas_call(
        combine_kernel,
        in_specs=whole(2),
        out_specs=whole(1)[0],
        out_shape=jax.ShapeDtypeStruct((tok_rows, feat_width), bf16),
        compiler_params=params(),
        name="combine",
    )(table, returned.reshape(EXPERTS * capacity, feat_width))
    block = outer_mean(keep, send, got)
    momentum_next, local_next, moe_out = outer_finish(moe_out, at, block, global_params, momentum, local_params)
    return (moe_out, momentum_next, local_next)


def solution(mesh):
    fine = Mesh(mesh.devices.reshape(4, 4, 2, 4, 2), REP + SHARD)
    in_specs = (
        P(REP + SHARD, None),
        P(REP + SHARD, None),
        P(REP + SHARD, None),
        P(SHARD, None, None),
        P(SHARD, None, None),
        P(SHARD, None, None),
        P(REP, SHARD, None),
        P(SHARD, None),
        P(SHARD, REP),
        P(REP, SHARD, None),
    )
    out_specs = (P(REP + SHARD, None), P(SHARD, REP), P(REP, SHARD, None))
    return jax.shard_map(local, mesh=fine, in_specs=in_specs, out_specs=out_specs, check_vma=False)
```
